512 devices in a mesh: gx: 4 (over x), gy: 8 (over y_lo, core), gz: 16 (over y_hi, z).
Axes of the slice: x: 4, y: 8 (y_hi: 2, y_lo: 4; y = y_hi * 4 + y_lo), z: 8, core: 2. Of those that a mesh axis runs over, the one named last changes fastest.
Arguments:
- positions: float32 [3, 16, 8, 64, 64], P(None, 'gz', 'gx', 'gy'), may hold values from 0 to 1
- counts: int32 [16, 8, 64], P('gz', 'gx', 'gy'), may hold values from 16 to 64, as said below
Outputs:
- force: float32 [3, 16, 8, 64, 64], P(None, 'gz', 'gx', 'gy')
- energy: float32 [16, 8, 64, 64], P('gz', 'gx', 'gy')
The draws below stay inside these ranges and needn't reach their ends.
Inputs may be any that keep to these rules, and one draw needn't show every extreme that they name: `counts`: every draw has some full cells.
All inputs are finite; a program needn't handle non-finite values.
Results may differ from the reference program's by a relative error of at most 0.0003.
Values sent between devices are 32-bit elements; how exact they have to be, the bound alone decides.
No kernel may reach another device: no remote copies, remote signals or barrier semaphores. Data moves between devices by JAX's collectives and lax.ppermute only.
A program may use at most 64 MiB of HBM per device.

```python
import jax
import jax.numpy as jnp
from jax import lax

SLOTS = 64
NX = 8
NY = 64
NZ = 16


def draw_counts(key, part):
    first = jax.random.fold_in(key, 11)
    second = jax.random.fold_in(key, 23)
    base = jax.random.randint(first, (NZ, NX, NY), SLOTS // 4, 3 * SLOTS // 4 + 1)
    full = jax.random.randint(second, (NZ, NX, NY), 0, 16) == 0
    counts = jnp.where(full, SLOTS, base)
    counts = counts.at[0, 0, 0].set(SLOTS)
    return counts.astype(jnp.int32)


def block_levels(rng, extent, shards, least, largest):
    loudness, own = 1.0, jax.random.fold_in(rng, 6)
    for position, blocks in shards:
        draws = jnp.exp(jax.random.uniform(jax.random.fold_in(own, position), (blocks,), jnp.float32, least / len(shards), largest / len(shards)))
        loudness = loudness * jnp.repeat(draws, extent[position] // blocks).reshape([-1 if axis == position else 1 for axis in range(len(extent))])
    return loudness


def setup_inputs(seed: int = 0) -> dict:
    keys = jax.random.split(jax.random.key(seed), 3)
    return {
        "positions": jnp.clip(1.0 * jax.random.uniform(keys[0], (3, NZ, NX, NY, SLOTS), jnp.float32) ** block_levels(keys[0], (3, NZ, NX, NY, SLOTS), ((1, 16), (2, 4), (3, 8)), -0.2, 0.2), 0.0, 1.0),
        "counts": draw_counts(jax.random.fold_in(keys[2], 71), 0),
    }


cutoff_sq = 4.95 * 4.95
cell_sides = (12.0, 12.0, 2.5)
density_width = 8.0
pair_width = 3.0
density_amp = 1.0
pair_amp = 2.0

def kernels(squared):
    inside = jnp.where(squared < cutoff_sq, 1.0 - squared / cutoff_sq, 0.0)
    smooth = inside * inside
    smooth_slope = -2.0 * inside / cutoff_sq
    first = jnp.exp(-squared / density_width)
    second = jnp.exp(-squared / pair_width)
    return (density_amp * first * smooth, density_amp * first * (smooth_slope - smooth / density_width), pair_amp * second * smooth, pair_amp * second * (smooth_slope - smooth / pair_width))

def neighbours(extended, centre_z, start_x, start_y, rows_x, rows_y, step_z, step_x):
    pieces = []
    for step_y in (-1, 0, 1):
        pieces.append(extended[:, centre_z + step_z, start_x + step_x:start_x + step_x + rows_x, start_y + step_y:start_y + step_y + rows_y])
    return jnp.concatenate(pieces, axis=-1)

def pair_geometry(center, partner, step_z, step_x, slots):
    lateral = (jnp.arange(3 * slots) // slots - 1).astype(jnp.float32)
    moves = (float(step_x), lateral, float(step_z))
    squared = jnp.zeros((), jnp.float32)
    deltas = []
    for component in range(3):
        delta = (center[component][..., :, None] - partner[component][..., None, :] - moves[component]) * cell_sides[component]
        deltas.append(delta)
        squared = squared + delta * delta
    weight = center[3][..., :, None] * partner[3][..., None, :]
    if step_z == 0 and step_x == 0:
        column = jnp.arange(3 * slots)[None, :]
        row_index = jnp.arange(slots)[:, None]
        weight = weight * (column != row_index + slots).astype(jnp.float32)
    return (deltas, squared, weight)

def densities(extended, centre_z, start_x, start_y, rows_x, rows_y, slots):
    center = extended[:, centre_z, start_x:start_x + rows_x, start_y:start_y + rows_y]
    summed = jnp.zeros(center.shape[1:], jnp.float32)
    for step_z in range(-2, 3):
        for step_x in range(-1, 2):
            partner = neighbours(extended, centre_z, start_x, start_y, rows_x, rows_y, step_z, step_x)
            deltas, squared, weight = pair_geometry(center, partner, step_z, step_x, slots)
            summed = summed + lax.optimization_barrier(jnp.sum(weight * kernels(squared)[0], axis=-1))
    return summed

def forces(extended, centre_z, rows_x, rows_y, slots):
    center = extended[:, centre_z, 1:1 + rows_x, 1:1 + rows_y]
    pushes = [jnp.zeros(center.shape[1:], jnp.float32) for component in range(3)]
    pairs = jnp.zeros(center.shape[1:], jnp.float32)
    for step_z in range(-2, 3):
        for step_x in range(-1, 2):
            partner = neighbours(extended, centre_z, 1, 1, rows_x, rows_y, step_z, step_x)
            deltas, squared, weight = pair_geometry(center, partner, step_z, step_x, slots)
            values = kernels(squared)
            factor = weight * ((center[4][..., :, None] + partner[4][..., None, :]) * values[1] + values[3])
            pushes = [pushes[component] - 2.0 * lax.optimization_barrier(jnp.sum(factor * deltas[component], axis=-1)) for component in range(3)]
            pairs = pairs + lax.optimization_barrier(jnp.sum(weight * values[2], axis=-1))
    return (jnp.stack(pushes), pairs)

def reference(positions, counts):
    occupied = (jnp.arange(SLOTS)[None, None, None, :] < counts[..., None]).astype(jnp.float32)
    stacked = jnp.concatenate([positions, occupied[None]], axis=0)

    def window(source, layer):
        layers = ((layer + jnp.arange(-2, 3)) % NZ).astype(jnp.int32)
        taken = jnp.take(source, layers, axis=1)
        return jnp.pad(taken, ((0, 0), (0, 0), (1, 1), (1, 1), (0, 0)), mode='wrap')

    def first_pass(layer):
        return densities(window(stacked, layer), 2, 1, 1, NX, NY, SLOTS)
    density = lax.map(first_pass, jnp.arange(NZ))
    root = jnp.sqrt(1.0 + density)
    slope = -0.5 / root
    full = jnp.concatenate([stacked, slope[None]], axis=0)

    def second_pass(layer):
        return forces(window(full, layer), 2, NX, NY, SLOTS)
    pushes, pairs = lax.map(second_pass, jnp.arange(NZ))
    force = jnp.moveaxis(pushes, 0, 1)
    energy = occupied * (-root + 0.5 * pairs)
    return (force, energy)
```

```python
import math

import jax
import jax.numpy as jnp
import ml_dtypes
import numpy as np
from jax import lax
from jax.experimental import pallas as pl
from jax.experimental.pallas import tpu as pltpu
from jax.sharding import PartitionSpec as P

SLOTS = 64
FAR = 100.0

cutoff_sq = 4.95 * 4.95
side_xy, side_z = 12.0, 2.5
KAPPA = math.log2(math.e) / 8.0
UNIT = math.sqrt(KAPPA)
TOP = KAPPA * cutoff_sq
RATIO = 8.0 / 3.0
DENSITY = 2.0 ** (-TOP) / TOP**2
PAIR = 2.0 ** (-TOP * RATIO)
SLOPE = 2.0 * 2.0 ** (-TOP) / TOP
G1, G2 = 2.0 / cutoff_sq, 1.0 / (8.0 * TOP)
H1, H2 = 4.0 * PAIR / TOP * 2.0 / cutoff_sq, 4.0 * PAIR / (3.0 * TOP * TOP)
PHI = 2.0 * PAIR / TOP**2

ROWS = 32
NY = 10
TERMS = 32
f32, bf16 = jnp.float32, jnp.bfloat16


def constants():
    lane = np.arange(256)
    off = np.zeros((ROWS, 256), np.float32)
    scale = np.zeros((ROWS, 256), np.float32)
    step = np.zeros((ROWS, 256), np.float32)
    off[0:10] = lane // SLOTS - 2
    off[10:20] = np.arange(10)[:, None] - 5
    off[20:30] = -0.5
    scale[0:20] = side_xy * UNIT
    scale[20:30] = side_z * UNIT
    step[20:30] = side_z * UNIT
    sel_b = np.zeros((NY, TERMS, 160), np.float32)
    sel_a = np.zeros((NY, TERMS, 160), np.float32)
    tops = []
    rest = np.float32(TOP)
    for _ in range(3):
        piece = rest.astype(ml_dtypes.bfloat16).astype(np.float32)
        tops.append(piece)
        rest = np.float32(rest - piece)
    for j in range(NY):
        row = 0
        for c in range(3):
            for pa, pb in ((0, 0), (0, 1), (0, 2), (1, 0), (1, 1), (2, 0)):
                sel_a[j, row, 32 * pa + 10 * c + j] = 2.0
                sel_b[j, row, 32 * pb + 10 * c + j] = 1.0
                row += 1
        for p in range(3):
            sel_a[j, row, 144] = -1.0
            sel_b[j, row, 96 + 16 * p + j] = 1.0
            row += 1
            sel_a[j, row, 96 + 16 * p + j] = -1.0
            sel_b[j, row, 144] = 1.0
            row += 1
            sel_a[j, row, 144] = tops[p]
            sel_b[j, row, 144] = 1.0
            row += 1
    outside = np.zeros((TERMS, 256), np.float32)
    outside[18] = 2.0**14
    return (
        off,
        scale,
        step,
        sel_b.reshape(NY * TERMS, 160).astype(ml_dtypes.bfloat16),
        sel_a.reshape(NY * TERMS, 160).astype(ml_dtypes.bfloat16),
        np.eye(256, dtype=np.float32).astype(ml_dtypes.bfloat16),
        outside.astype(ml_dtypes.bfloat16),
    )


def split3(x):
    a = x.astype(bf16)
    r = x - a.astype(f32)
    b = r.astype(bf16)
    c = (r - b.astype(f32)).astype(bf16)
    return a, b, c


def lanes_summed(rows):
    ones = jnp.ones((8, rows.shape[1]), f32)
    return lax.dot_general(
        ones,
        rows,
        (((1,), (1,)), ((), ())),
        precision=lax.Precision.HIGHEST,
        preferred_element_type=f32,
    )


def kernel(lo, mid, hi, off, scale, step, sel_b, sel_a, eye, outside, force, energy, R, B, A, ACC, COL, SUM, V):
    for l in range(9):
        raw = (lo, mid, hi)[l % 3][l // 3]
        v = (raw + off[...]) * scale[...] + float(l - 4) * step[...]
        sq = v * v
        n = sq + pltpu.roll(sq, ROWS - 10, 0) + pltpu.roll(sq, ROWS - 20, 0)
        pieces = jnp.concatenate(
            split3(v) + split3(n[:16]) + (jnp.ones((16, 256), bf16),), axis=0
        )
        partner = jnp.dot(sel_b[...], pieces, preferred_element_type=f32).astype(bf16)
        B[l, 0] = outside[...]
        B[l, NY + 1] = outside[...]
        for j in range(NY):
            B[l, j + 1] = partner[TERMS * j : TERMS * (j + 1)]
        if 2 <= l <= 6:
            V[...] = v
            centre = jnp.dot(sel_a[...], pieces, preferred_element_type=f32).astype(bf16)
            for j in range(NY):
                for c in range(3):
                    R[l - 2, j, c : c + 1, :] = V[10 * c + j : 10 * c + j + 1, :]
                A[l - 2, j] = lax.dot_general(
                    eye[...],
                    centre[TERMS * j : TERMS * (j + 1)],
                    (((1,), (1,)), ((), ())),
                    preferred_element_type=f32,
                ).astype(bf16)

    def density(l, j):
        for h in range(2):
            lhs = A[l, j, 64 * h : 64 * h + 192, :]
            total = jnp.zeros((192, 128), f32)
            for a in range(5):
                for c in range(3):
                    rhs = B[l + a, j + c, :, 128 * h : 128 * h + 128]
                    tau = jnp.maximum(jnp.dot(lhs, rhs, preferred_element_type=f32), 0.0)
                    total = total + tau * tau * jnp.exp2(tau)
            if h == 0:
                ACC[0:192] = total
                ACC[192:256] = jnp.zeros((64, 128), f32)
            else:
                ACC[64:256] += total
        summed = lanes_summed(ACC[...])[0:1]
        root = jnp.sqrt(jnp.maximum(summed * DENSITY, 0.5))
        R[l, j, 3:4, :] = (-0.5 * SLOPE) / root
        R[l, j, 4:5, :] = root

    @pl.loop(0, 5)
    def _(l):
        @pl.loop(0, NY)
        def _(j):
            density(l, j)

    @pl.loop(0, 8)
    def _(j):
        own = pltpu.roll(R[2, j + 1], 256 - 64, 1)[:, 0:128]
        COL[:, 0:8] = own.T

        @pl.loop(0, 8)
        def _(g):
            rows = pl.ds(pl.multiple_of(g * 16, 16), 16)
            cols = COL[rows, :]
            xp, yp, zp, sp = (jnp.broadcast_to(cols[:, i : i + 1], (16, 128)) for i in range(4))
            fx = fy = fz = ph = jnp.zeros((16, 128), f32)
            for a in range(5):
                for c in range(3):
                    for h in range(2):
                        ln = slice(128 * h, 128 * h + 128)
                        dx = xp - R[a, j + c, 0:1, ln]
                        dy = yp - R[a, j + c, 1:2, ln]
                        dz = zp - R[a, j + c, 2:3, ln]
                        slopes = sp + R[a, j + c, 3:4, ln]
                        tau = jnp.maximum(TOP - (dx * dx + dy * dy + dz * dz), 0.0)
                        u = jnp.exp2(tau) * tau
                        w = jnp.exp2(tau * RATIO) * tau
                        ph = ph + w * tau
                        push = slopes * (u * (G1 + G2 * tau)) + w * (H1 + H2 * tau)
                        fx = fx + push * dx
                        fy = fy + push * dy
                        fz = fz + push * dz
            for i, part in enumerate((fx, fy, fz, ph)):
                SUM[i, rows, :] = part

        occupied = own[0:1] < 0.5 * FAR * side_xy * UNIT
        for i in range(3):
            total = lanes_summed(SUM[i])[0:1] * (1.0 / UNIT)
            force[i, pl.ds(j, 1), :] = jnp.where(occupied, total, 0.0)
        pairs = lanes_summed(SUM[3])[0:1] * PHI - 2.0
        energy[pl.ds(j, 1), :] = jnp.where(occupied, 0.5 * pairs - own[4:5], 0.0)


def shifted(x, axis, distance):
    n = lax.axis_size(axis)
    return lax.ppermute(x, axis, [((i - distance) % n, i) for i in range(n)])


def local_step(lo, mid, hi, interpret=False):
    consts = [jnp.asarray(c) for c in constants()]
    vmem = pl.BlockSpec(memory_space=pltpu.VMEM)
    return pl.pallas_call(
        kernel,
        out_shape=(
            jax.ShapeDtypeStruct((3, 8, 128), f32),
            jax.ShapeDtypeStruct((8, 128), f32),
        ),
        in_specs=[vmem] * 10,
        out_specs=(vmem, vmem),
        scratch_shapes=[
            pltpu.VMEM((5, NY, 8, 256), f32),
            pltpu.VMEM((9, NY + 2, TERMS, 256), bf16),
            pltpu.VMEM((5, NY, 256, TERMS), bf16),
            pltpu.VMEM((256, 128), f32),
            pltpu.VMEM((128, 128), f32),
            pltpu.VMEM((4, 128, 128), f32),
            pltpu.VMEM((ROWS, 256), f32),
        ],
        compiler_params=pltpu.CompilerParams(vmem_limit_bytes=48 * 2**20),
        interpret=interpret,
    )(lo, mid, hi, *consts)


def body(positions, counts):
    empty = jnp.arange(SLOTS) >= counts[0][..., None]
    x = jnp.where(empty, FAR, positions[0, 0])
    own = jnp.stack([x, positions[1, 0], positions[2, 0]])
    own = jnp.swapaxes(own, 1, 2).reshape(3, 8, 128)
    before = shifted(own[:, 7:8], "gy", 1)
    after = shifted(own[:, 0:1], "gy", -1)
    own = jnp.concatenate([before, own, after], axis=1)
    before = shifted(own[:, :, 64:], "gx", 1)
    after = shifted(own[:, :, :64], "gx", -1)
    own = jnp.concatenate([before, own, after], axis=2).reshape(30, 256)
    own = jnp.pad(own, ((0, 2), (0, 0)))
    mid = jnp.stack([shifted(own, "gz", 3), own, shifted(own, "gz", -3)])
    lo = shifted(mid, "gz", 1)
    hi = shifted(mid, "gz", -1)
    force, energy = local_step(lo, mid, hi)
    force = jnp.swapaxes(force.reshape(3, 8, 2, 64), 1, 2)[:, None]
    energy = jnp.swapaxes(energy.reshape(8, 2, 64), 0, 1)[None]
    return force, energy


def solution(mesh):
    return jax.shard_map(
        body,
        mesh=mesh,
        in_specs=(P(None, "gz", "gx", "gy", None), P("gz", "gx", "gy")),
        out_specs=(P(None, "gz", "gx", "gy", None), P("gz", "gx", "gy", None)),
        check_vma=False,
    )
```

```python
import math

import jax
import jax.numpy as jnp
import ml_dtypes
import numpy as np
from jax import lax
from jax.experimental import pallas as pl
from jax.experimental.pallas import tpu as pltpu
from jax.sharding import PartitionSpec as P

SLOTS = 64
FAR = 100.0

cutoff_sq = 4.95 * 4.95
side_xy, side_z = 12.0, 2.5
KAPPA = math.log2(math.e) / 8.0
UNIT = math.sqrt(KAPPA)
TOP = KAPPA * cutoff_sq
RATIO = 8.0 / 3.0
DENSITY = 2.0 ** (-TOP) / TOP**2
PAIR = 2.0 ** (-TOP * RATIO)
SLOPE = 2.0 * 2.0 ** (-TOP) / TOP
G1, G2 = 2.0 / cutoff_sq, 1.0 / (8.0 * TOP)
H1, H2 = 4.0 * PAIR / TOP * 2.0 / cutoff_sq, 4.0 * PAIR / (3.0 * TOP * TOP)
PHI = 2.0 * PAIR / TOP**2

NY = 10
TILE = 16
LAYERS, MIDDLE = 9, 5
TERMS = 32
DEPTH = 13 * TILE
WINDOW, CHUNK, EXTRA = 768, 768, 128
UNROLL = 5
CAPACITY = LAYERS * 256 + WINDOW + EXTRA
EMPTY = FAR * side_xy * UNIT
BOX = (side_xy * UNIT, 4 * side_xy * UNIT, 0.5 * side_z * UNIT)
NEAR = TOP * 1.001
f32, bf16 = jnp.float32, jnp.bfloat16


def constants():
    sel_b = np.zeros((NY, TERMS, DEPTH), np.float32)
    sel_a = np.zeros((NY, TERMS, DEPTH), np.float32)
    tops = []
    rest = np.float32(TOP)
    for _ in range(3):
        piece = rest.astype(ml_dtypes.bfloat16).astype(np.float32)
        tops.append(piece)
        rest = np.float32(rest - piece)
    one = 12 * TILE
    for j in range(NY):
        row = 0
        for c in range(3):
            for pa, pb in ((0, 0), (0, 1), (0, 2), (1, 0), (1, 1), (2, 0)):
                sel_a[j, row, TILE * (3 * c + pa) + j] = 2.0
                sel_b[j, row, TILE * (3 * c + pb) + j] = 1.0
                row += 1
        for p in range(3):
            sel_a[j, row, one] = -1.0
            sel_b[j, row, TILE * (9 + p) + j] = 1.0
            row += 1
            sel_a[j, row, TILE * (9 + p) + j] = -1.0
            sel_b[j, row, one] = 1.0
            row += 1
            sel_a[j, row, one] = tops[p]
            sel_b[j, row, one] = 1.0
            row += 1
    across = np.zeros((DEPTH, NY, 128), np.float32)
    across[:, :, :TERMS] = sel_b.transpose(2, 0, 1)
    outside = np.zeros((WINDOW + EXTRA, TERMS), np.float32)
    outside[:, 18] = 2.0**14
    lane = np.arange(256)
    cast = lambda x: x.astype(ml_dtypes.bfloat16)
    return (
        cast(across.reshape(DEPTH, NY * 128)),
        cast(sel_a.reshape(NY * TERMS, DEPTH)),
        cast(np.eye(256, dtype=np.float32)),
        cast((lane[:, None] <= lane[None, :]).astype(np.float32)),
        cast(outside),
    )


def split3(x):
    a = x.astype(bf16)
    r = x - a.astype(f32)
    b = r.astype(bf16)
    c = (r - b.astype(f32)).astype(bf16)
    return (a, b, c)


def pieces(x, y, z):
    parts = split3(x) + split3(y) + split3(z) + split3(x * x + y * y + z * z)
    return jnp.concatenate(parts + (jnp.ones((TILE, x.shape[1]), bf16),), axis=0)


def lanes_summed(rows):
    ones = jnp.ones((8, rows.shape[1]), bf16)
    total = jnp.zeros((8, rows.shape[0]), f32)
    for part in split3(rows):
        total = total + lax.dot_general(
            ones, part, (((1,), (1,)), ((), ())), preferred_element_type=f32
        )
    return total


def across(x, index):
    return jnp.take_along_axis(x, index, axis=1)


def taken(x, index):
    low = across(x[:, :128], index & 127)
    high = across(x[:, 128:], index & 127)
    return jnp.where(index >= 128, high, low)


def packed(count, fields, group):
    place = lax.broadcasted_iota(jnp.int32, (TILE, 128), 1) + 128 * group
    want = place.astype(f32)
    low, high = count[:, :128], count[:, 128:]
    beyond = want >= low[:, 127:128]
    at = jnp.zeros((TILE, 128), jnp.int32)
    for step in (64, 32, 16, 8, 4, 2, 1):
        probe = at + (step - 1)
        seen = across(high, probe)
        if group == 0:
            seen = jnp.where(beyond, seen, across(low, probe))
        at = jnp.where(seen <= want, at + step, at)
    there = want < high[:, 127:128]
    found = []
    for field, blank in zip(fields, (EMPTY, 0.0, 0.0)):
        value = across(field[:, 128:], at)
        if group == 0:
            value = jnp.where(beyond, value, across(field[:, :128], at))
        found.append(jnp.where(there, value, blank))
    return found


def push_parts(centre, partner, sums):
    (xp, yp, zp, sp), (xq, yq, zq, sq), (fx, fy, fz, ph) = centre, partner, sums
    dx, dy, dz = xp - xq, yp - yq, zp - zq
    tau = jnp.maximum(TOP - (dx * dx + dy * dy + dz * dz), 0.0)
    u = jnp.exp2(tau) * tau
    w = jnp.exp2(tau * RATIO) * tau
    push = (sp + sq) * (u * (G1 + G2 * tau)) + w * (H1 + H2 * tau)
    return fx + push * dx, fy + push * dy, fz + push * dz, ph + w * tau


def kernel(
    at_z, recv, place_b, sel_a, eye, upto, outside, force, energy,
    COUNT, MASK, CUM, NUMS, OFF, XYZ, TURNED, P, C, D, SLOPE_D, ROOT_D, OWN, COL, SUM, RES, sem,
):
    SLOPE_D[...] = jnp.ones(SLOPE_D.shape, f32)
    row = lax.broadcasted_iota(jnp.int32, (TILE, 256), 0)
    cell = lax.broadcasted_iota(jnp.int32, (TILE, 256), 1) // SLOTS
    real = row < NY
    ring = recv.shape[0]

    for l in range(LAYERS):
        source = lax.rem(at_z[0] + (l + ring - 4), ring)
        raw = recv[source, 1 if l == LAYERS - 1 else 0]
        x = (raw[0:TILE] + (cell - 2).astype(f32)) * (side_xy * UNIT)
        y = (pltpu.roll(raw, 32 - NY, 0)[0:TILE] + (row - 5).astype(f32)) * (side_xy * UNIT)
        z = (pltpu.roll(raw, 32 - 2 * NY, 0)[0:TILE] + (l - 4.5)) * (side_z * UNIT)
        for c, value in enumerate((x, y, z)):
            XYZ[l, c] = value
        apart = [jnp.maximum(jnp.abs(v) - side, 0.0) for v, side in zip((x, y, z), BOX)]
        far = apart[0] * apart[0] + apart[1] * apart[1] + apart[2] * apart[2]
        mark = lambda test: jnp.where(real & test, 1.0, 0.0).astype(bf16)
        MASK[TILE * l : TILE * (l + 1)] = mark(far < 4.0 * NEAR)
        if 2 <= l <= 6:
            MASK[TILE * (l + 7) : TILE * (l + 8)] = mark(far < NEAR)
        if l == 4:
            inside = (cell >= 1) & (cell <= 2) & (row >= 1) & (row <= 8) & (x < 0.5 * EMPTY)
            MASK[TILE * 14 : TILE * 15] = mark(inside)
            MASK[TILE * 15 : TILE * 16] = jnp.zeros((TILE, 256), bf16)
    CUM[...] = jnp.dot(MASK[...], upto[...], preferred_element_type=f32)
    COUNT[...] = lax.dot_general(
        jnp.ones((8, 256), bf16), MASK[...], (((1,), (1,)), ((), ())), preferred_element_type=f32
    ).astype(jnp.int32)
    copy = pltpu.make_async_copy(COUNT, NUMS, sem)
    copy.start()

    for l in range(MIDDLE):
        count = CUM[TILE * (l + 9) : TILE * (l + 10)]
        fields = [XYZ[l + 2, c] for c in range(3)]
        groups = [packed(count, fields, w) for w in range(2)]
        for w in range(2):
            for c in range(3):
                D[l, c, w] = groups[w][c]
            terms = jnp.dot(sel_a[...], pieces(*groups[w]), preferred_element_type=f32).astype(bf16)
            for j in range(NY):
                C[l, j, w] = terms[TERMS * j : TERMS * (j + 1)]
    copy.wait()

    for j in range(NY + 2):
        start = jnp.int32(0)
        for l in range(LAYERS):
            OFF[l, j] = start
            if 1 <= j <= NY:
                start = start + ((NUMS[0, TILE * l + j - 1] + 15) >> 4 << 4)
        OFF[LAYERS, j] = start
    for l in range(LAYERS):
        count = CUM[TILE * l : TILE * (l + 1)]
        fields = [XYZ[l, c] for c in range(3)]
        both = [pieces(*packed(count, fields, w)) for w in range(2)]
        TURNED[256 * l : 256 * (l + 1)] = lax.dot_general(
            eye[...],
            jnp.concatenate(both, axis=1),
            (((1,), (1,)), ((), ())),
            preferred_element_type=f32,
        ).astype(bf16)
    for j in range(NY):
        place = place_b[:, 128 * j : 128 * (j + 1)]
        rows = jnp.dot(TURNED[...], place, preferred_element_type=f32)[:, :TERMS].astype(bf16)
        for l in range(LAYERS):
            start = pl.multiple_of(OFF[l, j + 1], 16)
            P[j + 1, pl.ds(start, 256), :] = rows[256 * l : 256 * (l + 1)]
    for j in range(NY + 2):
        P[j, pl.ds(pl.multiple_of(OFF[LAYERS, j], 16), WINDOW + EXTRA), :] = outside[...]

    def density(rows, lanes):
        tau = jnp.maximum(jnp.dot(rows, lanes, preferred_element_type=f32), 0.0)
        value = tau * tau * jnp.exp2(tau)
        return jnp.sum(value.reshape(-1, 8, 128), axis=0)

    def summed(l, j, w):
        total = jnp.zeros((8, 128), f32)
        for side in range(3):
            start = pl.multiple_of(OFF[l, j + side], 16)
            for part in range(0, WINDOW, CHUNK):
                at = pl.multiple_of(start + part, 16)
                total = total + density(P[j + side, pl.ds(at, CHUNK), :], C[l, j, w])
        SLOPE_D[l, w, pl.ds(j, 1), :] = jnp.sum(total, axis=0, keepdims=True)

    def rest(l, j, w):
        total = jnp.zeros((8, 128), f32)
        for side in range(3):
            start = OFF[l, j + side] + WINDOW
            more = jnp.maximum(OFF[l + MIDDLE, j + side] - start + EXTRA - 1, 0) // EXTRA

            def further(i, total):
                at = pl.multiple_of(start + i * EXTRA, 16)
                return total + density(P[j + side, pl.ds(at, EXTRA), :], C[l, j, w])

            total = lax.fori_loop(0, more, further, total)
        SLOPE_D[l, w, pl.ds(j, 1), :] += jnp.sum(total, axis=0, keepdims=True)

    @pl.loop(0, MIDDLE)
    def _(l):
        @pl.loop(0, NY, step=UNROLL)
        def _(first):
            for u in range(UNROLL):
                summed(l, first + u, 0)
            for u in range(UNROLL):
                j = first + u
                many = NUMS[0, TILE * (l + 9) + j] > 128
                longest = jnp.int32(0)
                for side in range(3):
                    longest = jnp.maximum(longest, OFF[l + MIDDLE, j + side] - OFF[l, j + side])

                @pl.when(many)
                def _(j=j):
                    summed(l, j, 1)

                @pl.when(longest > WINDOW)
                def _(j=j, many=many):
                    @pl.loop(0, jnp.where(many, 2, 1))
                    def _(w):
                        rest(l, j, w)

    root = jnp.sqrt(jnp.maximum(SLOPE_D[...] * DENSITY, 0.5))
    ROOT_D[...] = root
    SLOPE_D[...] = (-0.5 * SLOPE) / root

    count = CUM[TILE * 11 : TILE * 12]
    before = count[:, SLOTS - 1 : SLOTS].astype(jnp.int32)
    index = lax.broadcasted_iota(jnp.int32, (TILE, 128), 1) + before
    for c, pair in enumerate(
        [[D[2, c, w] for w in range(2)] for c in range(3)]
        + [[A[2, w] for w in range(2)] for A in (SLOPE_D, ROOT_D)]
    ):
        OWN[c] = taken(jnp.concatenate(pair, axis=1), index)

    def partner(l, j, w):
        one = pl.ds(j, 1)
        return (D[l, 0, w, one, :], D[l, 1, w, one, :], D[l, 2, w, one, :], SLOPE_D[l, w, one, :])

    def centre(j, rows):
        cols = COL[j, rows, :]
        return tuple(jnp.broadcast_to(cols[:, i : i + 1], (16, 128)) for i in range(4))

    @pl.loop(0, 8)
    def _(j):
        stack = jnp.concatenate([OWN[c, pl.ds(j + 1, 1), :] for c in range(4)] * 2, axis=0)
        COL[j, :, 0:8] = stack.T

        @pl.loop(0, (NUMS[0, TILE * 14 + j + 1] + 15) >> 4)
        def _(g):
            rows = pl.ds(pl.multiple_of(g * 16, 16), 16)
            mine = centre(j, rows)
            sums = (jnp.zeros((16, 128), f32),) * 4
            for l in range(MIDDLE):
                for side in range(3):
                    sums = push_parts(mine, partner(l, j + side, 0), sums)
            for i in range(4):
                SUM[j, i, rows, :] = sums[i]

    @pl.loop(0, MIDDLE)
    def _(l):
        @pl.loop(0, NY)
        def _(k):
            @pl.when(NUMS[0, TILE * (l + 9) + k] > 128)
            def _():
                @pl.loop(jnp.maximum(k - 2, 0), jnp.minimum(k + 1, 8))
                def _(j):
                    @pl.loop(0, (NUMS[0, TILE * 14 + j + 1] + 15) >> 4)
                    def _(g):
                        rows = pl.ds(pl.multiple_of(g * 16, 16), 16)
                        sums = tuple(SUM[j, i, rows, :] for i in range(4))
                        sums = push_parts(centre(j, rows), partner(l, k, 1), sums)
                        for i in range(4):
                            SUM[j, i, rows, :] = sums[i]

    for j in range(8):
        for i in range(4):
            RES[i, j : j + 1, :] = lanes_summed(SUM[j, i])[0:1]

    back = pltpu.roll(count, 256 - SLOTS, 1)[:, :128].astype(jnp.int32) - 1 - before
    back = jnp.concatenate([pltpu.roll(back, TILE - 1, 0)[0:8]], axis=0)
    occupied = pltpu.roll(XYZ[4, 0], 256 - SLOTS, 1)[:, :128]
    occupied = pltpu.roll(occupied, TILE - 1, 0)[0:8] < 0.5 * EMPTY
    back = jnp.where(occupied, back, 0)
    for i in range(3):
        force[i] = jnp.where(occupied, across(RES[i], back) * (1.0 / UNIT), 0.0)
    root = pltpu.roll(OWN[4], TILE - 1, 0)[0:8]
    energy[...] = jnp.where(occupied, across(RES[3] * (0.5 * PHI) - 1.0 - root, back), 0.0)


def local_step(at_z, recv, interpret=False):
    consts = [jnp.asarray(c) for c in constants()]
    vmem = pl.BlockSpec(memory_space=pltpu.VMEM)
    return pl.pallas_call(
        kernel,
        out_shape=(
            jax.ShapeDtypeStruct((3, 8, 128), f32),
            jax.ShapeDtypeStruct((8, 128), f32),
        ),
        in_specs=[pl.BlockSpec(memory_space=pltpu.SMEM)] + [vmem] * 6,
        out_specs=(vmem, vmem),
        scratch_shapes=[
            pltpu.VMEM((8, 256), jnp.int32),
            pltpu.VMEM((256, 256), bf16),
            pltpu.VMEM((256, 256), f32),
            pltpu.SMEM((8, 256), jnp.int32),
            pltpu.SMEM((LAYERS + 1, TILE), jnp.int32),
            pltpu.VMEM((LAYERS, 3, TILE, 256), f32),
            pltpu.VMEM((LAYERS * 256, DEPTH), bf16),
            pltpu.VMEM((NY + 2, CAPACITY, TERMS), bf16),
            pltpu.VMEM((MIDDLE, NY, 2, TERMS, 128), bf16),
            pltpu.VMEM((MIDDLE, 3, 2, TILE, 128), f32),
            pltpu.VMEM((MIDDLE, 2, TILE, 128), f32),
            pltpu.VMEM((MIDDLE, 2, TILE, 128), f32),
            pltpu.VMEM((5, TILE, 128), f32),
            pltpu.VMEM((8, 128, 128), f32),
            pltpu.VMEM((8, 4, 128, 128), f32),
            pltpu.VMEM((4, 8, 128), f32),
            pltpu.SemaphoreType.DMA,
        ],
        compiler_params=pltpu.CompilerParams(vmem_limit_bytes=48 * 2**20),
        interpret=interpret,
    )(at_z, recv, *consts)


def along(axis, ring, distance):
    n = lax.axis_size(axis)
    return [(i, i - i % ring + (i + distance) % ring) for i in range(n)]


def around_y(distance):
    nz, ny = lax.axis_size("gz"), lax.axis_size("gy")
    pairs = []
    for k in range(nz):
        for j in range(ny):
            there = j + distance
            layer = k if 0 <= there < ny else (k + nz // 2) % nz
            pairs.append((j * nz + k, (there % ny) * nz + layer))
    return pairs


def turned(pair, swap):
    return jnp.where(swap, pair[::-1], pair)


def gathered(positions, counts):
    nz = lax.axis_size("gz")
    half = nz // 2
    at_y, at_z = lax.axis_index("gy"), lax.axis_index("gz") % half
    last_y = lax.axis_size("gy") - 1
    empty = jnp.arange(SLOTS) >= counts[0][..., None]
    x = jnp.where(empty, FAR, positions[0, 0])
    own = jnp.stack([x, positions[1, 0], positions[2, 0]])
    own = jnp.swapaxes(own, 1, 2).reshape(3, 8, 128)
    other = lax.ppermute(own, "gz", along("gz", nz, half))
    both = jnp.stack([own, other])
    up = turned(both[:, :, 7:8], at_y == last_y)
    down = turned(both[:, :, 0:1], at_y == 0)
    before = lax.ppermute(up, ("gy", "gz"), around_y(1))
    after = lax.ppermute(down, ("gy", "gz"), around_y(-1))
    both = jnp.concatenate([before, both, after], axis=2)
    nx = lax.axis_size("gx")
    before = lax.ppermute(both[..., 64:], "gx", along("gx", nx, 1))
    after = lax.ppermute(both[..., :64], "gx", along("gx", nx, -1))
    both = jnp.concatenate([before, both, after], axis=3).reshape(2, 30, 256)
    both = jnp.pad(both, ((0, 0), (0, 2), (0, 0)))
    chunks = []
    for there in range(half):
        ahead = at_z - there
        first = (jnp.abs(ahead) < half // 2) | (ahead == -(half // 2))
        chunks.append(turned(both, ~first))
    groups = [list(range(half)), list(range(half, nz))]
    recv = lax.all_to_all(jnp.stack(chunks), "gz", 0, 0, axis_index_groups=groups)
    return at_z.astype(jnp.int32).reshape(1), recv


def body(positions, counts):
    force, energy = local_step(*gathered(positions, counts))
    force = jnp.swapaxes(force.reshape(3, 8, 2, 64), 1, 2)[:, None]
    energy = jnp.swapaxes(energy.reshape(8, 2, 64), 0, 1)[None]
    return force, energy


def solution(mesh):
    return jax.shard_map(
        body,
        mesh=mesh,
        in_specs=(P(None, "gz", "gx", "gy", None), P("gz", "gx", "gy")),
        out_specs=(P(None, "gz", "gx", "gy", None), P("gz", "gx", "gy", None)),
        check_vma=False,
    )
```

```python
import functools
import math

import jax
import jax.numpy as jnp
import ml_dtypes
import numpy as np
from jax import lax
from jax.experimental import pallas as pl
from jax.experimental.pallas import tpu as pltpu
from jax.sharding import PartitionSpec as P

SLOTS = 64
FAR = 100.0

cutoff_sq = 4.95 * 4.95
side_xy, side_z = 12.0, 2.5
KAPPA = math.log2(math.e) / 8.0
UNIT = math.sqrt(KAPPA)
TOP = KAPPA * cutoff_sq
RATIO = 8.0 / 3.0
DENSITY = 2.0 ** (-TOP) / TOP**2
PAIR = 2.0 ** (-TOP * RATIO)
SLOPE = 2.0 * 2.0 ** (-TOP) / TOP
G1, G2 = 2.0 / cutoff_sq, 1.0 / (8.0 * TOP)
H1, H2 = 4.0 * PAIR / TOP * 2.0 / cutoff_sq, 4.0 * PAIR / (3.0 * TOP * TOP)
PHI = 2.0 * PAIR / TOP**2

NY = 10
TILE = 16
LAYERS, MIDDLE = 9, 5
TERMS = 32
DEPTH = 13 * TILE
WINDOW, EDGE, EXTRA = 768, 512, 128
STEP = 16
CAPACITY = LAYERS * 256 + WINDOW + EXTRA
EMPTY = FAR * side_xy * UNIT
BOX = (side_xy * UNIT, 4 * side_xy * UNIT, 0.5 * side_z * UNIT)
NEAR = TOP * 1.001
f32, bf16 = jnp.float32, jnp.bfloat16


def constants():
    sel_b = np.zeros((NY, TERMS, DEPTH), np.float32)
    sel_a = np.zeros((NY, TERMS, DEPTH), np.float32)
    tops = []
    rest = np.float32(TOP)
    for _ in range(3):
        piece = rest.astype(ml_dtypes.bfloat16).astype(np.float32)
        tops.append(piece)
        rest = np.float32(rest - piece)
    one = 12 * TILE
    for j in range(NY):
        row = 0
        for c in range(3):
            for pa, pb in ((0, 0), (0, 1), (0, 2), (1, 0), (1, 1), (2, 0)):
                sel_a[j, row, TILE * (3 * c + pa) + j] = 2.0
                sel_b[j, row, TILE * (3 * c + pb) + j] = 1.0
                row += 1
        for p in range(3):
            sel_a[j, row, one] = -1.0
            sel_b[j, row, TILE * (9 + p) + j] = 1.0
            row += 1
            sel_a[j, row, TILE * (9 + p) + j] = -1.0
            sel_b[j, row, one] = 1.0
            row += 1
            sel_a[j, row, one] = tops[p]
            sel_b[j, row, one] = 1.0
            row += 1
    across = np.zeros((DEPTH, NY, 128), np.float32)
    across[:, :, :TERMS] = sel_b.transpose(2, 0, 1)
    outside = np.zeros((WINDOW + EXTRA, TERMS), np.float32)
    outside[:, 18] = 2.0**14
    lane = np.arange(256)
    cast = lambda x: x.astype(ml_dtypes.bfloat16)
    return (
        cast(across.reshape(DEPTH, NY * 128)),
        cast(sel_a.reshape(NY * TERMS, DEPTH)),
        cast(np.eye(256, dtype=np.float32)),
        cast((lane[:, None] <= lane[None, :]).astype(np.float32)),
        cast(outside),
    )


def split3(x):
    a = x.astype(bf16)
    r = x - a.astype(f32)
    b = r.astype(bf16)
    c = (r - b.astype(f32)).astype(bf16)
    return (a, b, c)


def pieces(x, y, z):
    parts = split3(x) + split3(y) + split3(z) + split3(x * x + y * y + z * z)
    return jnp.concatenate(parts + (jnp.ones((TILE, x.shape[1]), bf16),), axis=0)


def lanes_summed(rows):
    ones = jnp.ones((8, rows.shape[1]), bf16)
    total = jnp.zeros((8, rows.shape[0]), f32)
    for part in split3(rows):
        total = total + lax.dot_general(
            ones, part, (((1,), (1,)), ((), ())), preferred_element_type=f32
        )
    return total


def across(x, index):
    return jnp.take_along_axis(x, index, axis=1)


def taken(x, index):
    low = across(x[:, :128], index & 127)
    high = across(x[:, 128:], index & 127)
    return jnp.where(index >= 128, high, low)


def packed(count, fields, group):
    place = lax.broadcasted_iota(jnp.int32, (TILE, 128), 1) + 128 * group
    want = place.astype(f32)
    low, high = count[:, :128], count[:, 128:]
    beyond = want >= low[:, 127:128]
    at = jnp.zeros((TILE, 128), jnp.int32)
    for step in (64, 32, 16, 8, 4, 2, 1):
        probe = at + (step - 1)
        seen = across(high, probe)
        if group == 0:
            seen = jnp.where(beyond, seen, across(low, probe))
        at = jnp.where(seen <= want, at + step, at)
    there = want < high[:, 127:128]
    found = []
    for field, blank in zip(fields, (EMPTY, 0.0, 0.0)):
        value = across(field[:, 128:], at)
        if group == 0:
            value = jnp.where(beyond, value, across(field[:, :128], at))
        found.append(jnp.where(there, value, blank))
    return found


def push_parts(centre, partner, sums):
    (xp, yp, zp, sp), (xq, yq, zq, sq), (fx, fy, fz, ph) = centre, partner, sums
    dx, dy, dz = xp - xq, yp - yq, zp - zq
    tau = jnp.maximum(TOP - (dx * dx + dy * dy + dz * dz), 0.0)
    u = jnp.exp2(tau) * tau
    w = jnp.exp2(tau * RATIO) * tau
    push = (sp + sq) * (u * (G1 + G2 * tau)) + w * (H1 + H2 * tau)
    return fx + push * dx, fy + push * dy, fz + push * dz, ph + w * tau


def kernel(
    at_z, recv, place_b, sel_a, eye, upto, outside, force, energy,
    COUNT, MASK, CUM, NUMS, OFF, XYZ, TURNED, P, C, D, SLOPE_D, ROOT_D, OWN, LATE, COL, SUM, RES, sem,
):
    SLOPE_D[...] = jnp.ones(SLOPE_D.shape, f32)
    row = lax.broadcasted_iota(jnp.int32, (TILE, 256), 0)
    cell = lax.broadcasted_iota(jnp.int32, (TILE, 256), 1) // SLOTS
    real = row < NY
    ring = recv.shape[0]

    for l in range(LAYERS):
        raw = recv[lax.rem(at_z[0] + (l + ring - 4), ring)]
        x = (raw[0:TILE] + (cell - 2).astype(f32)) * (side_xy * UNIT)
        y = (pltpu.roll(raw, 32 - NY, 0)[0:TILE] + (row - 5).astype(f32)) * (side_xy * UNIT)
        z = (pltpu.roll(raw, 32 - 2 * NY, 0)[0:TILE] + (l - 4.5)) * (side_z * UNIT)
        for c, value in enumerate((x, y, z)):
            XYZ[l, c] = value
        apart = [jnp.maximum(jnp.abs(v) - side, 0.0) for v, side in zip((x, y, z), BOX)]
        far = apart[0] * apart[0] + apart[1] * apart[1] + apart[2] * apart[2]
        mark = lambda test: jnp.where(real & test, 1.0, 0.0).astype(bf16)
        MASK[TILE * l : TILE * (l + 1)] = mark(far < 4.0 * NEAR)
        if 2 <= l <= 6:
            MASK[TILE * (l + 7) : TILE * (l + 8)] = mark(far < NEAR)
        if l == 4:
            inside = (cell >= 1) & (cell <= 2) & (row >= 1) & (row <= 8) & (x < 0.5 * EMPTY)
            MASK[TILE * 14 : TILE * 15] = mark(inside)
            MASK[TILE * 15 : TILE * 16] = jnp.zeros((TILE, 256), bf16)
    CUM[...] = jnp.dot(MASK[...], upto[...], preferred_element_type=f32)
    COUNT[...] = lax.dot_general(
        jnp.ones((8, 256), bf16), MASK[...], (((1,), (1,)), ((), ())), preferred_element_type=f32
    ).astype(jnp.int32)
    copy = pltpu.make_async_copy(COUNT, NUMS, sem)
    copy.start()

    for l in range(MIDDLE):
        count = CUM[TILE * (l + 9) : TILE * (l + 10)]
        fields = [XYZ[l + 2, c] for c in range(3)]
        groups = [packed(count, fields, w) for w in range(2)]
        for w in range(2):
            for c in range(3):
                D[l, c, w] = groups[w][c]
            terms = jnp.dot(sel_a[...], pieces(*groups[w]), preferred_element_type=f32).astype(bf16)
            for j in range(NY):
                C[l, j, w] = terms[TERMS * j : TERMS * (j + 1)]
    copy.wait()

    for j in range(NY + 2):
        start = jnp.int32(0)
        for l in range(LAYERS):
            OFF[l, j] = start
            if 1 <= j <= NY:
                start = start + ((NUMS[0, TILE * l + j - 1] + 15) >> 4 << 4)
        OFF[LAYERS, j] = start
    for l in range(LAYERS):
        count = CUM[TILE * l : TILE * (l + 1)]
        fields = [XYZ[l, c] for c in range(3)]
        both = [pieces(*packed(count, fields, w)) for w in range(2)]
        TURNED[256 * l : 256 * (l + 1)] = lax.dot_general(
            eye[...],
            jnp.concatenate(both, axis=1),
            (((1,), (1,)), ((), ())),
            preferred_element_type=f32,
        ).astype(bf16)
    for j in range(NY):
        place = place_b[:, 128 * j : 128 * (j + 1)]
        rows = jnp.dot(TURNED[...], place, preferred_element_type=f32)[:, :TERMS].astype(bf16)
        for l in range(LAYERS):
            start = pl.multiple_of(OFF[l, j + 1], 16)
            P[j + 1, pl.ds(start, 256), :] = rows[256 * l : 256 * (l + 1)]
    for j in range(NY + 2):
        P[j, pl.ds(pl.multiple_of(OFF[LAYERS, j], 16), WINDOW + EXTRA), :] = outside[...]

    def density(rows, lanes):
        tau = jnp.maximum(jnp.dot(rows, lanes, preferred_element_type=f32), 0.0)
        value = tau * tau * jnp.exp2(tau)
        return jnp.sum(value.reshape(-1, 8, 128), axis=0)

    def summed(l, j, w):
        total = jnp.zeros((8, 128), f32)
        for k in range(max(j - 1, 0), min(j + 2, NY)):
            window = EDGE if k in (0, NY - 1) else WINDOW
            start = pl.multiple_of(OFF[l, k + 1], 16)
            total = total + density(P[k + 1, pl.ds(start, window), :], C[l, j, w])
        SLOPE_D[l, w, j : j + 1, :] = jnp.sum(total, axis=0, keepdims=True)

    def rest(l, j, w):
        total = jnp.zeros((8, 128), f32)
        for k in range(max(j - 1, 0), min(j + 2, NY)):
            start = OFF[l, k + 1] + (EDGE if k in (0, NY - 1) else WINDOW)
            more = jnp.maximum(OFF[l + MIDDLE, k + 1] - start + EXTRA - 1, 0) // EXTRA

            def further(i, total):
                at = pl.multiple_of(start + i * EXTRA, 16)
                return total + density(P[k + 1, pl.ds(at, EXTRA), :], C[l, j, w])

            total = lax.fori_loop(0, more, further, total)
        SLOPE_D[l, w, j : j + 1, :] += jnp.sum(total, axis=0, keepdims=True)

    @pl.loop(0, MIDDLE)
    def _(l):
        for j in range(NY):
            summed(l, j, 0)
        excess = []
        for k in range(NY):
            length = OFF[l + MIDDLE, k + 1] - OFF[l, k + 1]
            excess.append(length - (EDGE if k in (0, NY - 1) else WINDOW))
        for j in range(NY):
            many = NUMS[0, TILE * (l + 9) + j] > 128

            @pl.when(many)
            def _():
                summed(l, j, 1)

            most = functools.reduce(jnp.maximum, excess[max(j - 1, 0) : min(j + 2, NY)])

            @pl.when(most > 0)
            def _():
                @pl.loop(0, jnp.where(many, 2, 1))
                def _(w):
                    rest(l, j, w)

    root = jnp.sqrt(jnp.maximum(SLOPE_D[...] * DENSITY, 0.5))
    ROOT_D[...] = root
    SLOPE_D[...] = (-0.5 * SLOPE) / root

    count = CUM[TILE * 11 : TILE * 12]
    before = count[:, SLOTS - 1 : SLOTS].astype(jnp.int32)
    index = lax.broadcasted_iota(jnp.int32, (TILE, 128), 1) + before
    for c, pair in enumerate(
        [[D[2, c, w] for w in range(2)] for c in range(3)]
        + [[A[2, w] for w in range(2)] for A in (SLOPE_D, ROOT_D)]
    ):
        OWN[c] = taken(jnp.concatenate(pair, axis=1), index)

    start = jnp.zeros((TILE, 1), f32)
    place = lax.broadcasted_iota(jnp.int32, (TILE, 128), 1)
    for c in range(4):
        LATE[c] = jnp.full((TILE, 128), EMPTY if c == 0 else 0.0, f32)
    for l in range(MIDDLE):
        held = jnp.maximum(CUM[TILE * (l + 9) : TILE * (l + 10), 255:256] - 128.0, 0.0)
        held = jnp.broadcast_to(held, (TILE, 128))
        for side in range(3):
            n = pltpu.roll(held, (TILE + 1 - side) % TILE, 0)
            first = jnp.broadcast_to(start, (TILE, 128))
            ours = (place.astype(f32) >= first) & (place.astype(f32) < first + n)
            index = (place - first.astype(jnp.int32)) & 127
            for c, field in enumerate([D[l, c, 1] for c in range(3)] + [SLOPE_D[l, 1]]):
                field = pltpu.roll(field, (TILE + 1 - side) % TILE, 0)
                LATE[c] = jnp.where(ours, across(field, index), LATE[c])
            start = start + n[:, 0:1]
    inner = lax.broadcasted_iota(jnp.int32, (TILE, 1), 0)
    inner = (inner >= 1) & (inner <= 8)
    crowded = jnp.max(jnp.where(inner, start, 0.0)) > 128.0

    @pl.when(crowded)
    def _():
        LATE[0] = jnp.full((TILE, 128), EMPTY, f32)

    def partner(l, j, w):
        one = pl.ds(j, 1)
        return (D[l, 0, w, one, :], D[l, 1, w, one, :], D[l, 2, w, one, :], SLOPE_D[l, w, one, :])

    def centre(j, rows):
        cols = COL[j, rows, :]
        return tuple(jnp.broadcast_to(cols[:, i : i + 1], (STEP, 128)) for i in range(4))

    def steps(j):
        return (NUMS[0, TILE * 14 + j + 1] + STEP - 1) // STEP

    @pl.loop(0, 8)
    def _(j):
        stack = jnp.concatenate([OWN[c, pl.ds(j + 1, 1), :] for c in range(4)] * 2, axis=0)
        COL[j, :, 0:8] = stack.T

        @pl.loop(0, steps(j))
        def _(g):
            rows = pl.ds(pl.multiple_of(g * STEP, STEP), STEP)
            mine = centre(j, rows)
            sums = (jnp.zeros((STEP, 128), f32),) * 4
            for l in range(MIDDLE):
                for side in range(3):
                    sums = push_parts(mine, partner(l, j + side, 0), sums)
            late = tuple(LATE[c, pl.ds(j + 1, 1), :] for c in range(4))
            sums = push_parts(mine, late, sums)
            for i in range(4):
                SUM[j, i, rows, :] = sums[i]

    @pl.when(crowded)
    def _():
        @pl.loop(0, MIDDLE)
        def _(l):
            @pl.loop(0, NY)
            def _(k):
                @pl.loop(jnp.maximum(k - 2, 0), jnp.minimum(k + 1, 8))
                def _(j):
                    @pl.loop(0, steps(j))
                    def _(g):
                        rows = pl.ds(pl.multiple_of(g * STEP, STEP), STEP)
                        sums = tuple(SUM[j, i, rows, :] for i in range(4))
                        sums = push_parts(centre(j, rows), partner(l, k, 1), sums)
                        for i in range(4):
                            SUM[j, i, rows, :] = sums[i]

    for j in range(8):
        for i in range(4):
            RES[i, j : j + 1, :] = lanes_summed(SUM[j, i])[0:1]

    back = pltpu.roll(count, 256 - SLOTS, 1)[:, :128].astype(jnp.int32) - 1 - before
    back = jnp.concatenate([pltpu.roll(back, TILE - 1, 0)[0:8]], axis=0)
    occupied = pltpu.roll(XYZ[4, 0], 256 - SLOTS, 1)[:, :128]
    occupied = pltpu.roll(occupied, TILE - 1, 0)[0:8] < 0.5 * EMPTY
    back = jnp.where(occupied, back, 0)
    root = pltpu.roll(OWN[4], TILE - 1, 0)[0:8]
    values = [RES[i] * (1.0 / UNIT) for i in range(3)] + [RES[3] * (0.5 * PHI) - 1.0 - root]
    for i, value in enumerate(values):
        value = jnp.where(occupied, across(value, back), 0.0)
        for half, part in enumerate((value, pltpu.roll(value, SLOTS, 1))):
            if i < 3:
                force[i, half] = part[:, :SLOTS]
            else:
                energy[half] = part[:, :SLOTS]


def local_step(at_z, recv, interpret=False):
    consts = [jnp.asarray(c) for c in constants()]
    vmem = pl.BlockSpec(memory_space=pltpu.VMEM)
    return pl.pallas_call(
        kernel,
        out_shape=(
            jax.ShapeDtypeStruct((3, 2, 8, SLOTS), f32),
            jax.ShapeDtypeStruct((2, 8, SLOTS), f32),
        ),
        in_specs=[pl.BlockSpec(memory_space=pltpu.SMEM)] + [vmem] * 6,
        out_specs=(vmem, vmem),
        scratch_shapes=[
            pltpu.VMEM((8, 256), jnp.int32),
            pltpu.VMEM((256, 256), bf16),
            pltpu.VMEM((256, 256), f32),
            pltpu.SMEM((8, 256), jnp.int32),
            pltpu.SMEM((LAYERS + 1, TILE), jnp.int32),
            pltpu.VMEM((LAYERS, 3, TILE, 256), f32),
            pltpu.VMEM((LAYERS * 256, DEPTH), bf16),
            pltpu.VMEM((NY + 2, CAPACITY, TERMS), bf16),
            pltpu.VMEM((MIDDLE, NY, 2, TERMS, 128), bf16),
            pltpu.VMEM((MIDDLE, 3, 2, TILE, 128), f32),
            pltpu.VMEM((MIDDLE, 2, TILE, 128), f32),
            pltpu.VMEM((MIDDLE, 2, TILE, 128), f32),
            pltpu.VMEM((5, TILE, 128), f32),
            pltpu.VMEM((4, TILE, 128), f32),
            pltpu.VMEM((8, 128, 128), f32),
            pltpu.VMEM((8, 4, 128, 128), f32),
            pltpu.VMEM((4, 8, 128), f32),
            pltpu.SemaphoreType.DMA,
        ],
        compiler_params=pltpu.CompilerParams(vmem_limit_bytes=48 * 2**20),
        interpret=interpret,
    )(at_z, recv, *consts)


def along(axis, distance):
    n = lax.axis_size(axis)
    return [(i, (i + distance) % n) for i in range(n)]


def gathered(positions, counts):
    nz = lax.axis_size("gz")
    empty = jnp.arange(SLOTS) >= counts[0][..., None]
    x = jnp.where(empty, FAR, positions[0, 0])
    own = jnp.stack([x, positions[1, 0], positions[2, 0]])
    own = jnp.swapaxes(own, 1, 2).reshape(3, 8, 128)
    before = lax.ppermute(own[:, 7:8], "gy", along("gy", 1))
    after = lax.ppermute(own[:, 0:1], "gy", along("gy", -1))
    own = jnp.concatenate([before, own, after], axis=1)
    before = lax.ppermute(own[..., 64:], "gx", along("gx", 1))
    after = lax.ppermute(own[..., :64], "gx", along("gx", -1))
    own = jnp.concatenate([before, own, after], axis=2).reshape(30, 256)
    own = jnp.pad(own, ((0, 2), (0, 0)))
    recv = lax.all_to_all(jnp.broadcast_to(own, (nz, 32, 256)), "gz", 0, 0)
    return lax.axis_index("gz").astype(jnp.int32).reshape(1), recv


def body(positions, counts):
    force, energy = local_step(*gathered(positions, counts))
    return force[:, None], energy[None]


def solution(mesh):
    return jax.shard_map(
        body,
        mesh=mesh,
        in_specs=(P(None, "gz", "gx", "gy", None), P("gz", "gx", "gy")),
        out_specs=(P(None, "gz", "gx", "gy", None), P("gz", "gx", "gy", None)),
        check_vma=False,
    )
```

```python
import functools
import math

import jax
import jax.numpy as jnp
import ml_dtypes
import numpy as np
from jax import lax
from jax.experimental import pallas as pl
from jax.experimental.pallas import tpu as pltpu
from jax.sharding import PartitionSpec as P

SLOTS = 64
FAR = 100.0

cutoff_sq = 4.95 * 4.95
side_xy, side_z = 12.0, 2.5
KAPPA = math.log2(math.e) / 8.0
UNIT = math.sqrt(KAPPA)
TOP = KAPPA * cutoff_sq
RATIO = 8.0 / 3.0
DENSITY = 2.0 ** (-TOP) / TOP**2
PAIR = 2.0 ** (-TOP * RATIO)
G, H = 8.0 * 2.0 * TOP / cutoff_sq, 3.0 * 2.0 * TOP / cutoff_sq
FORCE = 4.0 * PAIR / (3.0 * TOP * TOP) / UNIT
SLOPE = 2.0 * 2.0 ** (-TOP) / (8.0 * TOP * TOP) / (FORCE * UNIT)
PHI = 2.0 * PAIR / TOP**2

NY = 10
TILE = 16
LAYERS, MIDDLE = 9, 5
TERMS = 32
DEPTH = 13 * TILE
WINDOW, EDGE, EXTRA = 704, 512, 128
STEP = 16
CAPACITY = LAYERS * 256 + WINDOW + EXTRA
EMPTY = FAR * side_xy * UNIT
BOX = (side_xy * UNIT, 4 * side_xy * UNIT, 0.5 * side_z * UNIT)
NEAR = TOP * 1.001
f32, bf16 = jnp.float32, jnp.bfloat16


def constants():
    sel_b = np.zeros((NY, TERMS, DEPTH), np.float32)
    sel_a = np.zeros((NY, TERMS, DEPTH), np.float32)
    tops = []
    rest = np.float32(TOP)
    for _ in range(3):
        piece = rest.astype(ml_dtypes.bfloat16).astype(np.float32)
        tops.append(piece)
        rest = np.float32(rest - piece)
    one = 12 * TILE
    for j in range(NY):
        row = 0
        for c in range(3):
            for pa, pb in ((0, 0), (0, 1), (0, 2), (1, 0), (1, 1), (2, 0)):
                sel_a[j, row, TILE * (3 * c + pa) + j] = 2.0
                sel_b[j, row, TILE * (3 * c + pb) + j] = 1.0
                row += 1
        for p in range(3):
            sel_a[j, row, one] = -1.0
            sel_b[j, row, TILE * (9 + p) + j] = 1.0
            row += 1
            sel_a[j, row, TILE * (9 + p) + j] = -1.0
            sel_b[j, row, one] = 1.0
            row += 1
            sel_a[j, row, one] = tops[p]
            sel_b[j, row, one] = 1.0
            row += 1
    across = np.zeros((DEPTH, NY, 128), np.float32)
    across[:, :, :TERMS] = sel_b.transpose(2, 0, 1)
    outside = np.zeros((WINDOW + EXTRA, TERMS), np.float32)
    outside[:, 18] = 2.0**14
    lane = np.arange(256)
    cast = lambda x: x.astype(ml_dtypes.bfloat16)
    return (
        cast(across.reshape(DEPTH, NY * 128)),
        cast(sel_a.reshape(NY * TERMS, DEPTH)),
        cast(np.eye(256, dtype=np.float32)),
        cast((lane[:, None] <= lane[None, :]).astype(np.float32)),
        cast(outside),
        cast((np.arange(512)[:, None] // 128 == lane[None, :128]).astype(np.float32)),
    )


def split3(x):
    a = x.astype(bf16)
    r = x - a.astype(f32)
    b = r.astype(bf16)
    c = (r - b.astype(f32)).astype(bf16)
    return (a, b, c)


def pieces(x, y, z):
    parts = split3(x) + split3(y) + split3(z) + split3(x * x + y * y + z * z)
    return jnp.concatenate(parts + (jnp.ones((TILE, x.shape[1]), bf16),), axis=0)


def across(x, index):
    return jnp.take_along_axis(x, index, axis=1)


def taken(x, index):
    low = across(x[:, :128], index & 127)
    high = across(x[:, 128:], index & 127)
    return jnp.where(index >= 128, high, low)


def packed(count, fields, group):
    place = lax.broadcasted_iota(jnp.int32, (TILE, 128), 1) + 128 * group
    want = place.astype(f32)
    low, high = count[:, :128], count[:, 128:]
    beyond = want >= low[:, 127:128]
    at = jnp.zeros((TILE, 128), jnp.int32)
    for step in (64, 32, 16, 8, 4, 2, 1):
        probe = at + (step - 1)
        seen = across(high, probe)
        if group == 0:
            seen = jnp.where(beyond, seen, across(low, probe))
        at = jnp.where(seen <= want, at + step, at)
    there = want < high[:, 127:128]
    found = []
    for field, blank in zip(fields, (EMPTY, 0.0, 0.0)):
        value = across(field[:, 128:], at)
        if group == 0:
            value = jnp.where(beyond, value, across(field[:, :128], at))
        found.append(jnp.where(there, value, blank))
    return found


def push_parts(centre, partner, sums):
    (xp, yp, zp, sp), (xq, yq, zq, sq), (fx, fy, fz, ph) = centre, partner, sums
    dx, dy, dz = xp - xq, yp - yq, zp - zq
    tau = jnp.maximum(TOP - (dx * dx + dy * dy + dz * dz), 0.0)
    w = jnp.exp2(tau * RATIO) * tau
    push = (sp + sq) * (jnp.exp2(tau) * tau * (tau + G)) + w * (tau + H)
    return fx + push * dx, fy + push * dy, fz + push * dz, ph + w * tau


def kernel(
    at_z, recv, place_b, sel_a, eye, upto, outside, add_up, force, energy,
    COUNT, MASK, CUM, NUMS, OFF, XYZ, TURNED, P, C, D, SLOPE_D, ROOT_D, OWN, LATE, COL, SUM, RES, sem,
):
    SLOPE_D[...] = jnp.ones(SLOPE_D.shape, f32)
    row = lax.broadcasted_iota(jnp.int32, (TILE, 256), 0)
    cell = lax.broadcasted_iota(jnp.int32, (TILE, 256), 1) // SLOTS
    real = row < NY
    ring = recv.shape[0]

    for l in range(LAYERS):
        raw = recv[lax.rem(at_z[0] + (l + ring - 4), ring)]
        x = (raw[0:TILE] + (cell - 2).astype(f32)) * (side_xy * UNIT)
        y = (pltpu.roll(raw, 32 - NY, 0)[0:TILE] + (row - 5).astype(f32)) * (side_xy * UNIT)
        z = (pltpu.roll(raw, 32 - 2 * NY, 0)[0:TILE] + (l - 4.5)) * (side_z * UNIT)
        for c, value in enumerate((x, y, z)):
            XYZ[l, c] = value
        apart = [jnp.maximum(jnp.abs(v) - side, 0.0) for v, side in zip((x, y, z), BOX)]
        far = apart[0] * apart[0] + apart[1] * apart[1] + apart[2] * apart[2]
        mark = lambda test: jnp.where(real & test, 1.0, 0.0).astype(bf16)
        MASK[TILE * l : TILE * (l + 1)] = mark(far < 4.0 * NEAR)
        if 2 <= l <= 6:
            MASK[TILE * (l + 7) : TILE * (l + 8)] = mark(far < NEAR)
        if l == 4:
            inside = (cell >= 1) & (cell <= 2) & (row >= 1) & (row <= 8) & (x < 0.5 * EMPTY)
            MASK[TILE * 14 : TILE * 15] = mark(inside)
            MASK[TILE * 15 : TILE * 16] = jnp.zeros((TILE, 256), bf16)
    CUM[...] = jnp.dot(MASK[...], upto[...], preferred_element_type=f32)
    COUNT[...] = lax.dot_general(
        jnp.ones((8, 256), bf16), MASK[...], (((1,), (1,)), ((), ())), preferred_element_type=f32
    ).astype(jnp.int32)
    copy = pltpu.make_async_copy(COUNT, NUMS, sem)
    copy.start()

    for l in range(MIDDLE):
        count = CUM[TILE * (l + 9) : TILE * (l + 10)]
        fields = [XYZ[l + 2, c] for c in range(3)]
        lists = [packed(count, fields, w) for w in range(2)]
        for w in range(2):
            for c in range(3):
                D[l, c, w] = lists[w][c]
        both = jnp.concatenate([pieces(*lists[w]) for w in range(2)], axis=1)
        terms = jnp.dot(sel_a[...], both, preferred_element_type=f32).astype(bf16)
        for j in range(NY):
            for w in range(2):
                C[l, j, w] = terms[TERMS * j : TERMS * (j + 1), 128 * w : 128 * (w + 1)]
    copy.wait()

    for j in range(NY + 2):
        start = jnp.int32(0)
        for l in range(LAYERS):
            OFF[l, j] = start
            if 1 <= j <= NY:
                start = start + ((NUMS[0, TILE * l + j - 1] + 15) >> 4 << 4)
        OFF[LAYERS, j] = start
    for l in range(LAYERS):
        count = CUM[TILE * l : TILE * (l + 1)]
        fields = [XYZ[l, c] for c in range(3)]
        both = [pieces(*packed(count, fields, w)) for w in range(2)]
        TURNED[256 * l : 256 * (l + 1)] = lax.dot_general(
            eye[...],
            jnp.concatenate(both, axis=1),
            (((1,), (1,)), ((), ())),
            preferred_element_type=f32,
        ).astype(bf16)
    for j in range(NY):
        place = place_b[:, 128 * j : 128 * (j + 1)]
        rows = jnp.dot(TURNED[...], place, preferred_element_type=f32)[:, :TERMS].astype(bf16)
        for l in range(LAYERS):
            start = pl.multiple_of(OFF[l, j + 1], 16)
            P[j + 1, pl.ds(start, 256), :] = rows[256 * l : 256 * (l + 1)]
    for j in range(NY + 2):
        P[j, pl.ds(pl.multiple_of(OFF[LAYERS, j], 16), WINDOW + EXTRA), :] = outside[...]

    def density(rows, lanes):
        tau = jnp.maximum(jnp.dot(rows, lanes, preferred_element_type=f32), 0.0)
        value = tau * tau * jnp.exp2(tau)
        return jnp.sum(value.reshape(-1, 8, 128), axis=0)

    def summed(l, j, w):
        total = jnp.zeros((8, 128), f32)
        for k in range(max(j - 1, 0), min(j + 2, NY)):
            window = EDGE if k in (0, NY - 1) else WINDOW
            start = pl.multiple_of(OFF[l, k + 1], 16)
            total = total + density(P[k + 1, pl.ds(start, window), :], C[l, j, w])
        SLOPE_D[l, w, j : j + 1, :] = jnp.sum(total, axis=0, keepdims=True)

    def rest(l, j, w):
        total = jnp.zeros((8, 128), f32)
        for k in range(max(j - 1, 0), min(j + 2, NY)):
            start = OFF[l, k + 1] + (EDGE if k in (0, NY - 1) else WINDOW)
            more = jnp.maximum(OFF[l + MIDDLE, k + 1] - start + EXTRA - 1, 0) // EXTRA

            def further(i, total):
                at = pl.multiple_of(start + i * EXTRA, 16)
                return total + density(P[k + 1, pl.ds(at, EXTRA), :], C[l, j, w])

            total = lax.fori_loop(0, more, further, total)
        SLOPE_D[l, w, j : j + 1, :] += jnp.sum(total, axis=0, keepdims=True)

    @pl.loop(0, MIDDLE)
    def _(l):
        for j in range(NY):
            summed(l, j, 0)
        excess = []
        for k in range(NY):
            length = OFF[l + MIDDLE, k + 1] - OFF[l, k + 1]
            excess.append(length - (EDGE if k in (0, NY - 1) else WINDOW))
        for j in range(NY):
            many = NUMS[0, TILE * (l + 9) + j] > 128

            @pl.when(many)
            def _():
                summed(l, j, 1)

            most = functools.reduce(jnp.maximum, excess[max(j - 1, 0) : min(j + 2, NY)])

            @pl.when(most > 0)
            def _():
                @pl.loop(0, jnp.where(many, 2, 1))
                def _(w):
                    rest(l, j, w)

    root = jnp.sqrt(jnp.maximum(SLOPE_D[...] * DENSITY, 0.5))
    ROOT_D[...] = root
    SLOPE_D[...] = (-0.5 * SLOPE) / root

    count = CUM[TILE * 11 : TILE * 12]
    before = count[:, SLOTS - 1 : SLOTS].astype(jnp.int32)
    index = lax.broadcasted_iota(jnp.int32, (TILE, 128), 1) + before
    for c, pair in enumerate(
        [[D[2, c, w] for w in range(2)] for c in range(3)]
        + [[A[2, w] for w in range(2)] for A in (SLOPE_D, ROOT_D)]
    ):
        OWN[c] = taken(jnp.concatenate(pair, axis=1), index)

    start = jnp.zeros((TILE, 1), f32)
    place = lax.broadcasted_iota(jnp.int32, (TILE, 128), 1)
    for c in range(4):
        LATE[c] = jnp.full((TILE, 128), EMPTY if c == 0 else 0.0, f32)
    for l in range(MIDDLE):
        held = jnp.maximum(CUM[TILE * (l + 9) : TILE * (l + 10), 255:256] - 128.0, 0.0)
        held = jnp.broadcast_to(held, (TILE, 128))
        for side in range(3):
            n = pltpu.roll(held, (TILE + 1 - side) % TILE, 0)
            first = jnp.broadcast_to(start, (TILE, 128))
            ours = (place.astype(f32) >= first) & (place.astype(f32) < first + n)
            index = (place - first.astype(jnp.int32)) & 127
            for c, field in enumerate([D[l, c, 1] for c in range(3)] + [SLOPE_D[l, 1]]):
                field = pltpu.roll(field, (TILE + 1 - side) % TILE, 0)
                LATE[c] = jnp.where(ours, across(field, index), LATE[c])
            start = start + n[:, 0:1]
    inner = lax.broadcasted_iota(jnp.int32, (TILE, 1), 0)
    inner = (inner >= 1) & (inner <= 8)
    crowded = jnp.max(jnp.where(inner, start, 0.0)) > 128.0

    @pl.when(crowded)
    def _():
        LATE[0] = jnp.full((TILE, 128), EMPTY, f32)

    def partner(l, j, w):
        one = pl.ds(j, 1)
        return (D[l, 0, w, one, :], D[l, 1, w, one, :], D[l, 2, w, one, :], SLOPE_D[l, w, one, :])

    def centre(j, rows):
        cols = COL[j, rows, :]
        return tuple(jnp.broadcast_to(cols[:, i : i + 1], (STEP, 128)) for i in range(4))

    def steps(j):
        return (NUMS[0, TILE * 14 + j + 1] + STEP - 1) // STEP

    @pl.loop(0, 8)
    def _(j):
        stack = jnp.concatenate([OWN[c, pl.ds(j + 1, 1), :] for c in range(4)] * 2, axis=0)
        COL[j, :, 0:8] = stack.T

        @pl.loop(0, steps(j))
        def _(g):
            rows = pl.ds(pl.multiple_of(g * STEP, STEP), STEP)
            mine = centre(j, rows)
            sums = (jnp.zeros((STEP, 128), f32),) * 4
            for l in range(MIDDLE):
                for side in range(3):
                    sums = push_parts(mine, partner(l, j + side, 0), sums)
            late = tuple(LATE[c, pl.ds(j + 1, 1), :] for c in range(4))
            sums = push_parts(mine, late, sums)
            for i in range(4):
                SUM[j, rows, 128 * i : 128 * (i + 1)] = sums[i]

    @pl.when(crowded)
    def _():
        @pl.loop(0, MIDDLE)
        def _(l):
            @pl.loop(0, NY)
            def _(k):
                some = jnp.where(NUMS[0, TILE * (l + 9) + k] > 128, 1, 0)

                @pl.loop(jnp.maximum(k - 2, 0), jnp.minimum(k + 1, 8))
                def _(j):
                    @pl.loop(0, steps(j) * some)
                    def _(g):
                        rows = pl.ds(pl.multiple_of(g * STEP, STEP), STEP)
                        sums = tuple(SUM[j, rows, 128 * i : 128 * (i + 1)] for i in range(4))
                        sums = push_parts(centre(j, rows), partner(l, k, 1), sums)
                        for i in range(4):
                            SUM[j, rows, 128 * i : 128 * (i + 1)] = sums[i]

    total = jnp.zeros((8 * 128, 128), f32)
    for part in split3(SUM[...].reshape(8 * 128, 4 * 128))[:2]:
        total = total + jnp.dot(part, add_up[...], preferred_element_type=f32)
    for j in range(8):
        across_lanes = total[128 * j : 128 * (j + 1), 0:8].T
        for i in range(4):
            RES[i, j : j + 1, :] = across_lanes[i : i + 1]

    back = pltpu.roll(count, 256 - SLOTS, 1)[:, :128].astype(jnp.int32) - 1 - before
    back = jnp.concatenate([pltpu.roll(back, TILE - 1, 0)[0:8]], axis=0)
    occupied = pltpu.roll(XYZ[4, 0], 256 - SLOTS, 1)[:, :128]
    occupied = pltpu.roll(occupied, TILE - 1, 0)[0:8] < 0.5 * EMPTY
    back = jnp.where(occupied, back, 0)
    root = pltpu.roll(OWN[4], TILE - 1, 0)[0:8]
    values = [RES[i] * FORCE for i in range(3)] + [RES[3] * (0.5 * PHI) - 1.0 - root]
    for i, value in enumerate(values):
        value = jnp.where(occupied, across(value, back), 0.0)
        for half, part in enumerate((value, pltpu.roll(value, SLOTS, 1))):
            if i < 3:
                force[i, half] = part[:, :SLOTS]
            else:
                energy[half] = part[:, :SLOTS]


def local_step(at_z, recv, interpret=False):
    consts = [jnp.asarray(c) for c in constants()]
    vmem = pl.BlockSpec(memory_space=pltpu.VMEM)
    return pl.pallas_call(
        kernel,
        out_shape=(
            jax.ShapeDtypeStruct((3, 2, 8, SLOTS), f32),
            jax.ShapeDtypeStruct((2, 8, SLOTS), f32),
        ),
        in_specs=[pl.BlockSpec(memory_space=pltpu.SMEM)] + [vmem] * 7,
        out_specs=(vmem, vmem),
        scratch_shapes=[
            pltpu.VMEM((8, 256), jnp.int32),
            pltpu.VMEM((256, 256), bf16),
            pltpu.VMEM((256, 256), f32),
            pltpu.SMEM((8, 256), jnp.int32),
            pltpu.SMEM((LAYERS + 1, TILE), jnp.int32),
            pltpu.VMEM((LAYERS, 3, TILE, 256), f32),
            pltpu.VMEM((LAYERS * 256, DEPTH), bf16),
            pltpu.VMEM((NY + 2, CAPACITY, TERMS), bf16),
            pltpu.VMEM((MIDDLE, NY, 2, TERMS, 128), bf16),
            pltpu.VMEM((MIDDLE, 3, 2, TILE, 128), f32),
            pltpu.VMEM((MIDDLE, 2, TILE, 128), f32),
            pltpu.VMEM((MIDDLE, 2, TILE, 128), f32),
            pltpu.VMEM((5, TILE, 128), f32),
            pltpu.VMEM((4, TILE, 128), f32),
            pltpu.VMEM((8, 128, 128), f32),
            pltpu.VMEM((8, 128, 512), f32),
            pltpu.VMEM((4, 8, 128), f32),
            pltpu.SemaphoreType.DMA,
        ],
        compiler_params=pltpu.CompilerParams(vmem_limit_bytes=48 * 2**20),
        interpret=interpret,
    )(at_z, recv, *consts)


def along(axis, distance):
    n = lax.axis_size(axis)
    return [(i, (i + distance) % n) for i in range(n)]


def marking_kernel(counts, positions, own, up, down):
    lane = lax.broadcasted_iota(jnp.int32, (1, SLOTS), 1)
    for i in range(2):
        lanes = slice(SLOTS * i, SLOTS * (i + 1))
        for j in range(8):
            row = jnp.where(lane < counts[0, i, j], positions[0, 0, i, j : j + 1, :], FAR)
            own[0, j : j + 1, lanes] = row
        for c in (1, 2):
            own[c, :, lanes] = positions[c, 0, i]
    for c in range(3):
        up[c] = own[c, 7:8]
        down[c] = own[c, 0:1]


def marked(positions, counts):
    vmem = pl.BlockSpec(memory_space=pltpu.VMEM)
    return pl.pallas_call(
        marking_kernel,
        out_shape=tuple(jax.ShapeDtypeStruct((3, n, 128), f32) for n in (8, 1, 1)),
        in_specs=[pl.BlockSpec(memory_space=pltpu.SMEM), vmem],
        out_specs=(vmem,) * 3,
    )(counts, positions)


def gathered(positions, counts):
    nz = lax.axis_size("gz")
    own, up, down = marked(positions, counts)
    before = lax.ppermute(up, "gy", along("gy", 1))
    after = lax.ppermute(down, "gy", along("gy", -1))
    own = jnp.concatenate([before, own, after], axis=1)
    before = lax.ppermute(own[..., 64:], "gx", along("gx", 1))
    after = lax.ppermute(own[..., :64], "gx", along("gx", -1))
    own = jnp.concatenate([before, own, after], axis=2).reshape(30, 256)
    own = jnp.pad(own, ((0, 2), (0, 0)))
    recv = lax.all_to_all(jnp.broadcast_to(own, (nz, 32, 256)), "gz", 0, 0)
    return lax.axis_index("gz").astype(jnp.int32).reshape(1), recv


def body(positions, counts):
    force, energy = local_step(*gathered(positions, counts))
    return force[:, None], energy[None]


def solution(mesh):
    return jax.shard_map(
        body,
        mesh=mesh,
        in_specs=(P(None, "gz", "gx", "gy", None), P("gz", "gx", "gy")),
        out_specs=(P(None, "gz", "gx", "gy", None), P("gz", "gx", "gy", None)),
        check_vma=False,
    )
```

```python
import functools
import math

import jax
import jax.numpy as jnp
import ml_dtypes
import numpy as np
from jax import lax
from jax.experimental import pallas as pl
from jax.experimental.pallas import tpu as pltpu
from jax.sharding import PartitionSpec as P

SLOTS = 64
FAR = 100.0

cutoff_sq = 4.95 * 4.95
side_xy, side_z = 12.0, 2.5
KAPPA = math.log2(math.e) / 8.0
UNIT = math.sqrt(KAPPA)
TOP = KAPPA * cutoff_sq
RATIO = 8.0 / 3.0
DENSITY = 2.0 ** (-TOP) / TOP**2
PAIR = 2.0 ** (-TOP * RATIO)
G, H = 8.0 * 2.0 * TOP / cutoff_sq, 3.0 * 2.0 * TOP / cutoff_sq
FORCE = 4.0 * PAIR / (3.0 * TOP * TOP) / UNIT
SLOPE = 2.0 * 2.0 ** (-TOP) / (8.0 * TOP * TOP) / (FORCE * UNIT)
PHI = 2.0 * PAIR / TOP**2

NY = 10
TILE = 16
LAYERS, MIDDLE = 9, 5
TERMS = 32
DEPTH = 13 * TILE
WINDOW, EDGE, EXTRA = 768, 576, 128
STEP = 16
CAPACITY = LAYERS * 256 + WINDOW + EXTRA
EMPTY = FAR * side_xy * UNIT
BOX = (side_xy * UNIT, 4 * side_xy * UNIT, 0.5 * side_z * UNIT)
NEAR = TOP * 1.001
f32, bf16 = jnp.float32, jnp.bfloat16


def constants():
    sel_b = np.zeros((NY, TERMS, DEPTH), np.float32)
    sel_a = np.zeros((NY, TERMS, DEPTH), np.float32)
    tops = []
    rest = np.float32(TOP)
    for _ in range(3):
        piece = rest.astype(ml_dtypes.bfloat16).astype(np.float32)
        tops.append(piece)
        rest = np.float32(rest - piece)
    one = 12 * TILE
    for j in range(NY):
        row = 0
        for c in range(3):
            for pa, pb in ((0, 0), (0, 1), (0, 2), (1, 0), (1, 1), (2, 0)):
                sel_a[j, row, TILE * (3 * c + pa) + j] = 2.0
                sel_b[j, row, TILE * (3 * c + pb) + j] = 1.0
                row += 1
        for p in range(3):
            sel_a[j, row, one] = -1.0
            sel_b[j, row, TILE * (9 + p) + j] = 1.0
            row += 1
            sel_a[j, row, TILE * (9 + p) + j] = -1.0
            sel_b[j, row, one] = 1.0
            row += 1
            sel_a[j, row, one] = tops[p]
            sel_b[j, row, one] = 1.0
            row += 1
    across = np.zeros((DEPTH, NY, 128), np.float32)
    across[:, :, :TERMS] = sel_b.transpose(2, 0, 1)
    outside = np.zeros((WINDOW + EXTRA, TERMS), np.float32)
    outside[:, 18] = 2.0**14
    lane = np.arange(256)
    cast = lambda x: x.astype(ml_dtypes.bfloat16)
    return (
        cast(across.reshape(DEPTH, NY * 128)),
        cast(sel_a.reshape(NY * TERMS, DEPTH)),
        cast(np.eye(256, dtype=np.float32)),
        cast((lane[:, None] <= lane[None, :]).astype(np.float32)),
        cast(outside),
        cast((np.arange(512)[:, None] // 128 == lane[None, :128]).astype(np.float32)),
    )


def split3(x):
    a = x.astype(bf16)
    r = x - a.astype(f32)
    b = r.astype(bf16)
    c = (r - b.astype(f32)).astype(bf16)
    return (a, b, c)


def pieces(x, y, z):
    parts = split3(x) + split3(y) + split3(z) + split3(x * x + y * y + z * z)
    return jnp.concatenate(parts + (jnp.ones((TILE, x.shape[1]), bf16),), axis=0)


def across(x, index):
    return jnp.take_along_axis(x, index, axis=1)


def taken(x, index):
    low = across(x[:, :128], index & 127)
    high = across(x[:, 128:], index & 127)
    return jnp.where(index >= 128, high, low)


def packed(count, fields, group):
    place = lax.broadcasted_iota(jnp.int32, (TILE, 128), 1) + 128 * group
    want = place.astype(f32)
    low, high = count[:, :128], count[:, 128:]
    beyond = want >= low[:, 127:128]
    at = jnp.zeros((TILE, 128), jnp.int32)
    for step in (64, 32, 16, 8, 4, 2, 1):
        probe = at + (step - 1)
        seen = across(high, probe)
        if group == 0:
            seen = jnp.where(beyond, seen, across(low, probe))
        at = jnp.where(seen <= want, at + step, at)
    there = want < high[:, 127:128]
    found = []
    for field, blank in zip(fields, (EMPTY, 0.0, 0.0)):
        value = across(field[:, 128:], at)
        if group == 0:
            value = jnp.where(beyond, value, across(field[:, :128], at))
        found.append(jnp.where(there, value, blank))
    return found


def push_parts(centre, partner, sums):
    (xp, yp, zp, sp), (xq, yq, zq, sq), (fx, fy, fz, ph) = centre, partner, sums
    dx, dy, dz = xp - xq, yp - yq, zp - zq
    tau = jnp.maximum(TOP - (dx * dx + dy * dy + dz * dz), 0.0)
    w = jnp.exp2(tau * RATIO) * tau
    push = (sp + sq) * (jnp.exp2(tau) * tau * (tau + G)) + w * (tau + H)
    return fx + push * dx, fy + push * dy, fz + push * dz, ph + w * tau


def kernel(
    at_z, recv, place_b, sel_a, eye, upto, outside, add_up, force, energy,
    COUNT, MASK, CUM, NUMS, OFF, XYZ, TURNED, P, C, D, SLOPE_D, ROOT_D, OWN, LATE, COL, SUM, RES, sem,
):
    SLOPE_D[...] = jnp.ones(SLOPE_D.shape, f32)
    row = lax.broadcasted_iota(jnp.int32, (TILE, 256), 0)
    cell = lax.broadcasted_iota(jnp.int32, (TILE, 256), 1) // SLOTS
    real = row < NY
    ring = recv.shape[0]

    for l in range(LAYERS):
        raw = recv[lax.rem(at_z[0] + (l + ring - 4), ring)]
        x = (raw[0:TILE] + (cell - 2).astype(f32)) * (side_xy * UNIT)
        y = (pltpu.roll(raw, 32 - NY, 0)[0:TILE] + (row - 5).astype(f32)) * (side_xy * UNIT)
        z = (pltpu.roll(raw, 32 - 2 * NY, 0)[0:TILE] + (l - 4.5)) * (side_z * UNIT)
        for c, value in enumerate((x, y, z)):
            XYZ[l, c] = value
        apart = [jnp.maximum(jnp.abs(v) - side, 0.0) for v, side in zip((x, y, z), BOX)]
        far = apart[0] * apart[0] + apart[1] * apart[1] + apart[2] * apart[2]
        mark = lambda test: jnp.where(real & test, 1.0, 0.0).astype(bf16)
        MASK[TILE * l : TILE * (l + 1)] = mark(far < 4.0 * NEAR)
        if 2 <= l <= 6:
            MASK[TILE * (l + 7) : TILE * (l + 8)] = mark(far < NEAR)
        if l == 4:
            inside = (cell >= 1) & (cell <= 2) & (row >= 1) & (row <= 8) & (x < 0.5 * EMPTY)
            MASK[TILE * 14 : TILE * 15] = mark(inside)
            MASK[TILE * 15 : TILE * 16] = jnp.zeros((TILE, 256), bf16)
    CUM[...] = jnp.dot(MASK[...], upto[...], preferred_element_type=f32)
    COUNT[...] = lax.dot_general(
        jnp.ones((8, 256), bf16), MASK[...], (((1,), (1,)), ((), ())), preferred_element_type=f32
    ).astype(jnp.int32)
    copy = pltpu.make_async_copy(COUNT, NUMS, sem)
    copy.start()

    for l in range(MIDDLE):
        count = CUM[TILE * (l + 9) : TILE * (l + 10)]
        fields = [XYZ[l + 2, c] for c in range(3)]
        lists = [packed(count, fields, w) for w in range(2)]
        for w in range(2):
            for c in range(3):
                D[l, c, w] = lists[w][c]
        both = jnp.concatenate([pieces(*lists[w]) for w in range(2)], axis=1)
        terms = jnp.dot(sel_a[...], both, preferred_element_type=f32).astype(bf16)
        for j in range(NY):
            for w in range(2):
                C[l, j, w] = terms[TERMS * j : TERMS * (j + 1), 128 * w : 128 * (w + 1)]
    copy.wait()

    for j in range(NY + 2):
        start = jnp.int32(0)
        for l in range(LAYERS):
            OFF[l, j] = start
            if 1 <= j <= NY:
                start = start + ((NUMS[0, TILE * l + j - 1] + 15) >> 4 << 4)
        OFF[LAYERS, j] = start
    for l in range(LAYERS):
        count = CUM[TILE * l : TILE * (l + 1)]
        fields = [XYZ[l, c] for c in range(3)]
        both = [pieces(*packed(count, fields, w)) for w in range(2)]
        TURNED[256 * l : 256 * (l + 1)] = lax.dot_general(
            eye[...],
            jnp.concatenate(both, axis=1),
            (((1,), (1,)), ((), ())),
            preferred_element_type=f32,
        ).astype(bf16)
    for j in range(NY):
        place = place_b[:, 128 * j : 128 * (j + 1)]
        rows = jnp.dot(TURNED[...], place, preferred_element_type=f32)[:, :TERMS].astype(bf16)
        for l in range(LAYERS):
            start = pl.multiple_of(OFF[l, j + 1], 16)
            P[j + 1, pl.ds(start, 256), :] = rows[256 * l : 256 * (l + 1)]
    for j in range(NY + 2):
        P[j, pl.ds(pl.multiple_of(OFF[LAYERS, j], 16), WINDOW + EXTRA), :] = outside[...]

    def density(rows, lanes):
        tau = jnp.maximum(jnp.dot(rows, lanes, preferred_element_type=f32), 0.0)
        value = tau * tau * jnp.exp2(tau)
        return jnp.sum(value.reshape(-1, 8, 128), axis=0)

    def summed(l, j, w):
        total = jnp.zeros((8, 128), f32)
        for k in range(max(j - 1, 0), min(j + 2, NY)):
            window = EDGE if k in (0, NY - 1) else WINDOW
            start = pl.multiple_of(OFF[l, k + 1], 16)
            total = total + density(P[k + 1, pl.ds(start, window), :], C[l, j, w])
        SLOPE_D[l, w, j : j + 1, :] = jnp.sum(total, axis=0, keepdims=True)

    def rest(l, j, w):
        total = jnp.zeros((8, 128), f32)
        for k in range(max(j - 1, 0), min(j + 2, NY)):
            start = OFF[l, k + 1] + (EDGE if k in (0, NY - 1) else WINDOW)
            more = jnp.maximum(OFF[l + MIDDLE, k + 1] - start + EXTRA - 1, 0) // EXTRA

            def further(i, total):
                at = pl.multiple_of(start + i * EXTRA, 16)
                return total + density(P[k + 1, pl.ds(at, EXTRA), :], C[l, j, w])

            total = lax.fori_loop(0, more, further, total)
        SLOPE_D[l, w, j : j + 1, :] += jnp.sum(total, axis=0, keepdims=True)

    @pl.loop(0, MIDDLE)
    def _(l):
        for j in range(NY):
            summed(l, j, 0)
        excess = []
        for k in range(NY):
            length = OFF[l + MIDDLE, k + 1] - OFF[l, k + 1]
            excess.append(length - (EDGE if k in (0, NY - 1) else WINDOW))
        for j in range(NY):
            many = NUMS[0, TILE * (l + 9) + j] > 128

            @pl.when(many)
            def _():
                summed(l, j, 1)

            most = functools.reduce(jnp.maximum, excess[max(j - 1, 0) : min(j + 2, NY)])

            @pl.when(most > 0)
            def _():
                @pl.loop(0, jnp.where(many, 2, 1))
                def _(w):
                    rest(l, j, w)

    root = jnp.sqrt(jnp.maximum(SLOPE_D[...] * DENSITY, 0.5))
    ROOT_D[...] = root
    SLOPE_D[...] = (-0.5 * SLOPE) / root

    count = CUM[TILE * 11 : TILE * 12]
    before = count[:, SLOTS - 1 : SLOTS].astype(jnp.int32)
    index = lax.broadcasted_iota(jnp.int32, (TILE, 128), 1) + before
    for c, pair in enumerate(
        [[D[2, c, w] for w in range(2)] for c in range(3)]
        + [[A[2, w] for w in range(2)] for A in (SLOPE_D, ROOT_D)]
    ):
        OWN[c] = taken(jnp.concatenate(pair, axis=1), index)

    start = jnp.zeros((TILE, 1), f32)
    place = lax.broadcasted_iota(jnp.int32, (TILE, 128), 1)
    for c in range(4):
        LATE[c] = jnp.full((TILE, 128), EMPTY if c == 0 else 0.0, f32)
    for l in range(MIDDLE):
        held = jnp.maximum(CUM[TILE * (l + 9) : TILE * (l + 10), 255:256] - 128.0, 0.0)
        held = jnp.broadcast_to(held, (TILE, 128))
        for side in range(3):
            n = pltpu.roll(held, (TILE + 1 - side) % TILE, 0)
            first = jnp.broadcast_to(start, (TILE, 128))
            ours = (place.astype(f32) >= first) & (place.astype(f32) < first + n)
            index = (place - first.astype(jnp.int32)) & 127
            for c, field in enumerate([D[l, c, 1] for c in range(3)] + [SLOPE_D[l, 1]]):
                field = pltpu.roll(field, (TILE + 1 - side) % TILE, 0)
                LATE[c] = jnp.where(ours, across(field, index), LATE[c])
            start = start + n[:, 0:1]
    inner = lax.broadcasted_iota(jnp.int32, (TILE, 1), 0)
    inner = (inner >= 1) & (inner <= 8)
    crowded = jnp.max(jnp.where(inner, start, 0.0)) > 128.0

    @pl.when(crowded)
    def _():
        LATE[0] = jnp.full((TILE, 128), EMPTY, f32)

    def partner(l, j, w):
        one = pl.ds(j, 1)
        return (D[l, 0, w, one, :], D[l, 1, w, one, :], D[l, 2, w, one, :], SLOPE_D[l, w, one, :])

    def centre(j, rows):
        cols = COL[j, rows, :]
        return tuple(jnp.broadcast_to(cols[:, i : i + 1], (STEP, 128)) for i in range(4))

    def steps(j):
        return (NUMS[0, TILE * 14 + j + 1] + STEP - 1) // STEP

    @pl.loop(0, 8)
    def _(j):
        stack = jnp.concatenate([OWN[c, pl.ds(j + 1, 1), :] for c in range(4)] * 2, axis=0)
        COL[j, :, 0:8] = stack.T

        @pl.loop(0, steps(j))
        def _(g):
            rows = pl.ds(pl.multiple_of(g * STEP, STEP), STEP)
            mine = centre(j, rows)
            sums = (jnp.zeros((STEP, 128), f32),) * 4
            for l in range(MIDDLE):
                for side in range(3):
                    sums = push_parts(mine, partner(l, j + side, 0), sums)
            late = tuple(LATE[c, pl.ds(j + 1, 1), :] for c in range(4))
            sums = push_parts(mine, late, sums)
            for i in range(4):
                SUM[j, rows, 128 * i : 128 * (i + 1)] = sums[i]

    @pl.when(crowded)
    def _():
        @pl.loop(0, MIDDLE)
        def _(l):
            @pl.loop(0, NY)
            def _(k):
                some = jnp.where(NUMS[0, TILE * (l + 9) + k] > 128, 1, 0)

                @pl.loop(jnp.maximum(k - 2, 0), jnp.minimum(k + 1, 8))
                def _(j):
                    @pl.loop(0, steps(j) * some)
                    def _(g):
                        rows = pl.ds(pl.multiple_of(g * STEP, STEP), STEP)
                        sums = tuple(SUM[j, rows, 128 * i : 128 * (i + 1)] for i in range(4))
                        sums = push_parts(centre(j, rows), partner(l, k, 1), sums)
                        for i in range(4):
                            SUM[j, rows, 128 * i : 128 * (i + 1)] = sums[i]

    total = jnp.zeros((8 * 128, 128), f32)
    for part in split3(SUM[...].reshape(8 * 128, 4 * 128))[:2]:
        total = total + jnp.dot(part, add_up[...], preferred_element_type=f32)
    for j in range(8):
        across_lanes = total[128 * j : 128 * (j + 1), 0:8].T
        for i in range(4):
            RES[i, j : j + 1, :] = across_lanes[i : i + 1]

    back = pltpu.roll(count, 256 - SLOTS, 1)[:, :128].astype(jnp.int32) - 1 - before
    back = jnp.concatenate([pltpu.roll(back, TILE - 1, 0)[0:8]], axis=0)
    occupied = pltpu.roll(XYZ[4, 0], 256 - SLOTS, 1)[:, :128]
    occupied = pltpu.roll(occupied, TILE - 1, 0)[0:8] < 0.5 * EMPTY
    back = jnp.where(occupied, back, 0)
    root = pltpu.roll(OWN[4], TILE - 1, 0)[0:8]
    values = [RES[i] * FORCE for i in range(3)] + [RES[3] * (0.5 * PHI) - 1.0 - root]
    for i, value in enumerate(values):
        value = jnp.where(occupied, across(value, back), 0.0)
        for half, part in enumerate((value, pltpu.roll(value, SLOTS, 1))):
            if i < 3:
                force[i, half] = part[:, :SLOTS]
            else:
                energy[half] = part[:, :SLOTS]


def local_step(at_z, recv, interpret=False):
    consts = [jnp.asarray(c) for c in constants()]
    vmem = pl.BlockSpec(memory_space=pltpu.VMEM)
    return pl.pallas_call(
        kernel,
        out_shape=(
            jax.ShapeDtypeStruct((3, 2, 8, SLOTS), f32),
            jax.ShapeDtypeStruct((2, 8, SLOTS), f32),
        ),
        in_specs=[pl.BlockSpec(memory_space=pltpu.SMEM)] + [vmem] * 7,
        out_specs=(vmem, vmem),
        scratch_shapes=[
            pltpu.VMEM((8, 256), jnp.int32),
            pltpu.VMEM((256, 256), bf16),
            pltpu.VMEM((256, 256), f32),
            pltpu.SMEM((8, 256), jnp.int32),
            pltpu.SMEM((LAYERS + 1, TILE), jnp.int32),
            pltpu.VMEM((LAYERS, 3, TILE, 256), f32),
            pltpu.VMEM((LAYERS * 256, DEPTH), bf16),
            pltpu.VMEM((NY + 2, CAPACITY, TERMS), bf16),
            pltpu.VMEM((MIDDLE, NY, 2, TERMS, 128), bf16),
            pltpu.VMEM((MIDDLE, 3, 2, TILE, 128), f32),
            pltpu.VMEM((MIDDLE, 2, TILE, 128), f32),
            pltpu.VMEM((MIDDLE, 2, TILE, 128), f32),
            pltpu.VMEM((5, TILE, 128), f32),
            pltpu.VMEM((4, TILE, 128), f32),
            pltpu.VMEM((8, 128, 128), f32),
            pltpu.VMEM((8, 128, 512), f32),
            pltpu.VMEM((4, 8, 128), f32),
            pltpu.SemaphoreType.DMA,
        ],
        compiler_params=pltpu.CompilerParams(vmem_limit_bytes=48 * 2**20),
        interpret=interpret,
    )(at_z, recv, *consts)


def along(axis, distance):
    n = lax.axis_size(axis)
    return [(i, (i + distance) % n) for i in range(n)]


def marking_kernel(counts, positions, own, up, down):
    lane = lax.broadcasted_iota(jnp.int32, (1, SLOTS), 1)
    for i in range(2):
        lanes = slice(SLOTS * i, SLOTS * (i + 1))
        for j in range(8):
            row = jnp.where(lane < counts[0, i, j], positions[0, 0, i, j : j + 1, :], FAR)
            own[0, j : j + 1, lanes] = row
        for c in (1, 2):
            own[c, :, lanes] = positions[c, 0, i]
    for c in range(3):
        up[c] = own[c, 7:8]
        down[c] = own[c, 0:1]


def marked(positions, counts):
    vmem = pl.BlockSpec(memory_space=pltpu.VMEM)
    return pl.pallas_call(
        marking_kernel,
        out_shape=tuple(jax.ShapeDtypeStruct((3, n, 128), f32) for n in (8, 1, 1)),
        in_specs=[pl.BlockSpec(memory_space=pltpu.SMEM), vmem],
        out_specs=(vmem,) * 3,
    )(counts, positions)


def gathered(positions, counts):
    nz = lax.axis_size("gz")
    own, up, down = marked(positions, counts)
    before = lax.ppermute(up, "gy", along("gy", 1))
    after = lax.ppermute(down, "gy", along("gy", -1))
    own = jnp.concatenate([before, own, after], axis=1)
    before = lax.ppermute(own[..., 64:], "gx", along("gx", 1))
    after = lax.ppermute(own[..., :64], "gx", along("gx", -1))
    own = jnp.concatenate([before, own, after], axis=2).reshape(30, 256)
    own = jnp.pad(own, ((0, 2), (0, 0)))
    recv = lax.all_to_all(jnp.broadcast_to(own, (nz, 32, 256)), "gz", 0, 0)
    return lax.axis_index("gz").astype(jnp.int32).reshape(1), recv


def body(positions, counts):
    force, energy = local_step(*gathered(positions, counts))
    return force[:, None], energy[None]


def solution(mesh):
    return jax.shard_map(
        body,
        mesh=mesh,
        in_specs=(P(None, "gz", "gx", "gy", None), P("gz", "gx", "gy")),
        out_specs=(P(None, "gz", "gx", "gy", None), P("gz", "gx", "gy", None)),
        check_vma=False,
    )
```

```python
import functools
import math

import jax
import jax.numpy as jnp
import ml_dtypes
import numpy as np
from jax import lax
from jax.experimental import pallas as pl
from jax.experimental.pallas import tpu as pltpu
from jax.sharding import PartitionSpec as P

SLOTS = 64
FAR = 100.0

cutoff_sq = 4.95 * 4.95
side_xy, side_z = 12.0, 2.5
KAPPA = math.log2(math.e) / 8.0
UNIT = math.sqrt(KAPPA)
TOP = KAPPA * cutoff_sq
RATIO = 8.0 / 3.0
DENSITY = 2.0 ** (-TOP) / TOP**2
PAIR = 2.0 ** (-TOP * RATIO)
G, H = 8.0 * 2.0 * TOP / cutoff_sq, 3.0 * 2.0 * TOP / cutoff_sq
FORCE = 4.0 * PAIR / (3.0 * TOP * TOP) / UNIT
SLOPE = 2.0 * 2.0 ** (-TOP) / (8.0 * TOP * TOP) / (FORCE * UNIT)
PHI = 2.0 * PAIR / TOP**2

NY = 10
TILE = 16
LAYERS, MIDDLE = 9, 5
TERMS = 32
DEPTH = 13 * TILE
WINDOW, EDGE, EXTRA = 768, 576, 128
STEP = 16
CAPACITY = LAYERS * 256 + WINDOW + EXTRA
EMPTY = FAR * side_xy * UNIT
BOX = (side_xy * UNIT, 4 * side_xy * UNIT, 0.5 * side_z * UNIT)
NEAR = TOP * 1.001
f32, bf16 = jnp.float32, jnp.bfloat16


def constants():
    sel_b = np.zeros((NY, TERMS, DEPTH), np.float32)
    sel_a = np.zeros((NY, TERMS, DEPTH), np.float32)
    tops = []
    rest = np.float32(TOP)
    for _ in range(3):
        piece = rest.astype(ml_dtypes.bfloat16).astype(np.float32)
        tops.append(piece)
        rest = np.float32(rest - piece)
    one = 12 * TILE
    for j in range(NY):
        row = 0
        for c in range(3):
            for pa, pb in ((0, 0), (0, 1), (0, 2), (1, 0), (1, 1), (2, 0)):
                sel_a[j, row, TILE * (3 * c + pa) + j] = 2.0
                sel_b[j, row, TILE * (3 * c + pb) + j] = 1.0
                row += 1
        for p in range(3):
            sel_a[j, row, one] = -1.0
            sel_b[j, row, TILE * (9 + p) + j] = 1.0
            row += 1
            sel_a[j, row, TILE * (9 + p) + j] = -1.0
            sel_b[j, row, one] = 1.0
            row += 1
            sel_a[j, row, one] = tops[p]
            sel_b[j, row, one] = 1.0
            row += 1
    across = np.zeros((DEPTH, NY, 128), np.float32)
    across[:, :, :TERMS] = sel_b.transpose(2, 0, 1)
    outside = np.zeros((WINDOW + EXTRA, TERMS), np.float32)
    outside[:, 18] = 2.0**14
    lane = np.arange(256)
    cast = lambda x: x.astype(ml_dtypes.bfloat16)
    return (
        cast(across.reshape(DEPTH, NY * 128)),
        cast(sel_a.reshape(NY * TERMS, DEPTH)),
        cast(np.eye(256, dtype=np.float32)),
        cast((lane[:, None] <= lane[None, :]).astype(np.float32)),
        cast(outside),
        cast((np.arange(512)[:, None] // 128 == lane[None, :128]).astype(np.float32)),
    )


def split3(x):
    a = x.astype(bf16)
    r = x - a.astype(f32)
    b = r.astype(bf16)
    c = (r - b.astype(f32)).astype(bf16)
    return (a, b, c)


def pieces(x, y, z):
    parts = split3(x) + split3(y) + split3(z) + split3(x * x + y * y + z * z)
    return jnp.concatenate(parts + (jnp.ones((TILE, x.shape[1]), bf16),), axis=0)


def across(x, index):
    return jnp.take_along_axis(x, index, axis=1)


def taken(x, index):
    low = across(x[:, :128], index & 127)
    high = across(x[:, 128:], index & 127)
    return jnp.where(index >= 128, high, low)


def packed(count, fields, group):
    place = lax.broadcasted_iota(jnp.int32, (TILE, 128), 1) + 128 * group
    want = place.astype(f32)
    low, high = count[:, :128], count[:, 128:]
    beyond = want >= low[:, 127:128]
    at = jnp.zeros((TILE, 128), jnp.int32)
    for step in (64, 32, 16, 8, 4, 2, 1):
        probe = at + (step - 1)
        seen = across(high, probe)
        if group == 0:
            seen = jnp.where(beyond, seen, across(low, probe))
        at = jnp.where(seen <= want, at + step, at)
    there = want < high[:, 127:128]
    found = []
    for field, blank in zip(fields, (EMPTY, 0.0, 0.0)):
        value = across(field[:, 128:], at)
        if group == 0:
            value = jnp.where(beyond, value, across(field[:, :128], at))
        found.append(jnp.where(there, value, blank))
    return found


def push_parts(centre, partner, sums):
    (xp, yp, zp, sp), (xq, yq, zq, sq), (fx, fy, fz, ph) = centre, partner, sums
    dx, dy, dz = xp - xq, yp - yq, zp - zq
    tau = jnp.maximum(TOP - (dx * dx + dy * dy + dz * dz), 0.0)
    w = jnp.exp2(tau * RATIO) * tau
    push = (sp + sq) * (jnp.exp2(tau) * tau * (tau + G)) + w * (tau + H)
    return fx + push * dx, fy + push * dy, fz + push * dz, ph + w * tau


def kernel(
    at_z, recv, place_b, sel_a, eye, upto, outside, add_up, force, energy,
    COUNT, MASK, CUM, NUMS, OFF, XYZ, TURNED, P, C, D, SLOPE_D, ROOT_D, OWN, LATE, COL, SUM, RES, sem,
):
    SLOPE_D[...] = jnp.ones(SLOPE_D.shape, f32)
    row = lax.broadcasted_iota(jnp.int32, (TILE, 256), 0)
    cell = lax.broadcasted_iota(jnp.int32, (TILE, 256), 1) // SLOTS
    real = row < NY
    ring = recv.shape[0]

    for l in range(LAYERS):
        raw = recv[lax.rem(at_z[0] + (l + ring - 4), ring)]
        x = (raw[0:TILE] + (cell - 2).astype(f32)) * (side_xy * UNIT)
        y = (pltpu.roll(raw, 32 - NY, 0)[0:TILE] + (row - 5).astype(f32)) * (side_xy * UNIT)
        z = (pltpu.roll(raw, 32 - 2 * NY, 0)[0:TILE] + (l - 4.5)) * (side_z * UNIT)
        for c, value in enumerate((x, y, z)):
            XYZ[l, c] = value
        apart = [jnp.maximum(jnp.abs(v) - side, 0.0) for v, side in zip((x, y, z), BOX)]
        far = apart[0] * apart[0] + apart[1] * apart[1] + apart[2] * apart[2]
        mark = lambda test: jnp.where(real & test, 1.0, 0.0).astype(bf16)
        MASK[TILE * l : TILE * (l + 1)] = mark(far < 4.0 * NEAR)
        if 2 <= l <= 6:
            MASK[TILE * (l + 7) : TILE * (l + 8)] = mark(far < NEAR)
        if l == 4:
            inside = (cell >= 1) & (cell <= 2) & (row >= 1) & (row <= 8) & (x < 0.5 * EMPTY)
            MASK[TILE * 14 : TILE * 15] = mark(inside)
            MASK[TILE * 15 : TILE * 16] = jnp.zeros((TILE, 256), bf16)
    CUM[...] = jnp.dot(MASK[...], upto[...], preferred_element_type=f32)
    COUNT[...] = lax.dot_general(
        jnp.ones((8, 256), bf16), MASK[...], (((1,), (1,)), ((), ())), preferred_element_type=f32
    ).astype(jnp.int32)
    copy = pltpu.make_async_copy(COUNT, NUMS, sem)
    copy.start()

    for l in range(MIDDLE):
        count = CUM[TILE * (l + 9) : TILE * (l + 10)]
        fields = [XYZ[l + 2, c] for c in range(3)]
        lists = [packed(count, fields, w) for w in range(2)]
        for w in range(2):
            for c in range(3):
                D[l, c, w] = lists[w][c]
        both = jnp.concatenate([pieces(*lists[w]) for w in range(2)], axis=1)
        terms = jnp.dot(sel_a[...], both, preferred_element_type=f32).astype(bf16)
        for j in range(NY):
            for w in range(2):
                C[l, j, w] = terms[TERMS * j : TERMS * (j + 1), 128 * w : 128 * (w + 1)]
    copy.wait()

    for j in range(NY + 2):
        start = jnp.int32(0)
        for l in range(LAYERS):
            OFF[l, j] = start
            if 1 <= j <= NY:
                start = start + ((NUMS[0, TILE * l + j - 1] + 15) >> 4 << 4)
        OFF[LAYERS, j] = start
    for l in range(LAYERS):
        count = CUM[TILE * l : TILE * (l + 1)]
        fields = [XYZ[l, c] for c in range(3)]
        both = [pieces(*packed(count, fields, w)) for w in range(2)]
        TURNED[256 * l : 256 * (l + 1)] = lax.dot_general(
            eye[...],
            jnp.concatenate(both, axis=1),
            (((1,), (1,)), ((), ())),
            preferred_element_type=f32,
        ).astype(bf16)
    for j in range(NY):
        place = place_b[:, 128 * j : 128 * (j + 1)]
        rows = jnp.dot(TURNED[...], place, preferred_element_type=f32)[:, :TERMS].astype(bf16)
        for l in range(LAYERS):
            start = pl.multiple_of(OFF[l, j + 1], 16)
            P[j + 1, pl.ds(start, 256), :] = rows[256 * l : 256 * (l + 1)]
    for j in range(NY + 2):
        P[j, pl.ds(pl.multiple_of(OFF[LAYERS, j], 16), WINDOW + EXTRA), :] = outside[...]

    def density(rows, lanes):
        tau = jnp.maximum(jnp.dot(rows, lanes, preferred_element_type=f32), 0.0)
        value = tau * tau * jnp.exp2(tau)
        return jnp.sum(value.reshape(-1, 8, 128), axis=0)

    def summed(l, j, w):
        total = jnp.zeros((8, 128), f32)
        for k in range(max(j - 1, 0), min(j + 2, NY)):
            window = EDGE if k in (0, NY - 1) else WINDOW
            start = pl.multiple_of(OFF[l, k + 1], 16)
            total = total + density(P[k + 1, pl.ds(start, window), :], C[l, j, w])
        SLOPE_D[l, w, j : j + 1, :] = jnp.sum(total, axis=0, keepdims=True)

    def rest(l, j, w):
        total = jnp.zeros((8, 128), f32)
        for k in range(max(j - 1, 0), min(j + 2, NY)):
            start = OFF[l, k + 1] + (EDGE if k in (0, NY - 1) else WINDOW)
            more = jnp.maximum(OFF[l + MIDDLE, k + 1] - start + EXTRA - 1, 0) // EXTRA

            def further(i, total):
                at = pl.multiple_of(start + i * EXTRA, 16)
                return total + density(P[k + 1, pl.ds(at, EXTRA), :], C[l, j, w])

            total = lax.fori_loop(0, more, further, total)
        SLOPE_D[l, w, j : j + 1, :] += jnp.sum(total, axis=0, keepdims=True)

    @pl.loop(0, MIDDLE)
    def _(l):
        for j in range(NY):
            summed(l, j, 0)
        excess = []
        for k in range(NY):
            length = OFF[l + MIDDLE, k + 1] - OFF[l, k + 1]
            excess.append(length - (EDGE if k in (0, NY - 1) else WINDOW))
        for j in range(NY):
            many = NUMS[0, TILE * (l + 9) + j] > 128

            @pl.when(many)
            def _():
                summed(l, j, 1)

            most = functools.reduce(jnp.maximum, excess[max(j - 1, 0) : min(j + 2, NY)])

            @pl.when(most > 0)
            def _():
                @pl.loop(0, jnp.where(many, 2, 1))
                def _(w):
                    rest(l, j, w)

    root = jnp.sqrt(jnp.maximum(SLOPE_D[...] * DENSITY, 0.5))
    ROOT_D[...] = root
    SLOPE_D[...] = (-0.5 * SLOPE) / root

    count = CUM[TILE * 11 : TILE * 12]
    before = count[:, SLOTS - 1 : SLOTS].astype(jnp.int32)
    index = lax.broadcasted_iota(jnp.int32, (TILE, 128), 1) + before
    for c, pair in enumerate(
        [[D[2, c, w] for w in range(2)] for c in range(3)]
        + [[A[2, w] for w in range(2)] for A in (SLOPE_D, ROOT_D)]
    ):
        OWN[c] = taken(jnp.concatenate(pair, axis=1), index)

    start = jnp.zeros((TILE, 1), f32)
    place = lax.broadcasted_iota(jnp.int32, (TILE, 128), 1)
    for c in range(4):
        LATE[c] = jnp.full((TILE, 128), EMPTY if c == 0 else 0.0, f32)
    for l in range(MIDDLE):
        held = jnp.maximum(CUM[TILE * (l + 9) : TILE * (l + 10), 255:256] - 128.0, 0.0)
        held = jnp.broadcast_to(held, (TILE, 128))
        for side in range(3):
            n = pltpu.roll(held, (TILE + 1 - side) % TILE, 0)
            first = jnp.broadcast_to(start, (TILE, 128))
            ours = (place.astype(f32) >= first) & (place.astype(f32) < first + n)
            index = (place - first.astype(jnp.int32)) & 127
            for c, field in enumerate([D[l, c, 1] for c in range(3)] + [SLOPE_D[l, 1]]):
                field = pltpu.roll(field, (TILE + 1 - side) % TILE, 0)
                LATE[c] = jnp.where(ours, across(field, index), LATE[c])
            start = start + n[:, 0:1]
    inner = lax.broadcasted_iota(jnp.int32, (TILE, 1), 0)
    inner = (inner >= 1) & (inner <= 8)
    crowded = jnp.max(jnp.where(inner, start, 0.0)) > 128.0

    @pl.when(crowded)
    def _():
        LATE[0] = jnp.full((TILE, 128), EMPTY, f32)

    def partner(l, j, w):
        one = pl.ds(j, 1)
        return (D[l, 0, w, one, :], D[l, 1, w, one, :], D[l, 2, w, one, :], SLOPE_D[l, w, one, :])

    def centre(j, rows):
        cols = COL[j, rows, :]
        return tuple(jnp.broadcast_to(cols[:, i : i + 1], (STEP, 128)) for i in range(4))

    def steps(j):
        return (NUMS[0, TILE * 14 + j + 1] + STEP - 1) // STEP

    @pl.loop(0, 8)
    def _(j):
        stack = jnp.concatenate([OWN[c, pl.ds(j + 1, 1), :] for c in range(4)] * 2, axis=0)
        COL[j, :, 0:8] = stack.T

        @pl.loop(0, steps(j))
        def _(g):
            rows = pl.ds(pl.multiple_of(g * STEP, STEP), STEP)
            mine = centre(j, rows)
            sums = (jnp.zeros((STEP, 128), f32),) * 4
            for l in range(MIDDLE):
                for side in range(3):
                    sums = push_parts(mine, partner(l, j + side, 0), sums)
            late = tuple(LATE[c, pl.ds(j + 1, 1), :] for c in range(4))
            sums = push_parts(mine, late, sums)
            for i in range(4):
                SUM[j, rows, 128 * i : 128 * (i + 1)] = sums[i]

    @pl.when(crowded)
    def _():
        @pl.loop(0, MIDDLE)
        def _(l):
            @pl.loop(0, NY)
            def _(k):
                some = jnp.where(NUMS[0, TILE * (l + 9) + k] > 128, 1, 0)

                @pl.loop(jnp.maximum(k - 2, 0), jnp.minimum(k + 1, 8))
                def _(j):
                    @pl.loop(0, steps(j) * some)
                    def _(g):
                        rows = pl.ds(pl.multiple_of(g * STEP, STEP), STEP)
                        sums = tuple(SUM[j, rows, 128 * i : 128 * (i + 1)] for i in range(4))
                        sums = push_parts(centre(j, rows), partner(l, k, 1), sums)
                        for i in range(4):
                            SUM[j, rows, 128 * i : 128 * (i + 1)] = sums[i]

    total = jnp.zeros((8 * 128, 128), f32)
    for part in split3(SUM[...].reshape(8 * 128, 4 * 128))[:2]:
        total = total + jnp.dot(part, add_up[...], preferred_element_type=f32)
    for j in range(8):
        across_lanes = total[128 * j : 128 * (j + 1), 0:8].T
        for i in range(4):
            RES[i, j : j + 1, :] = across_lanes[i : i + 1]

    back = pltpu.roll(count, 256 - SLOTS, 1)[:, :128].astype(jnp.int32) - 1 - before
    back = jnp.concatenate([pltpu.roll(back, TILE - 1, 0)[0:8]], axis=0)
    occupied = pltpu.roll(XYZ[4, 0], 256 - SLOTS, 1)[:, :128]
    occupied = pltpu.roll(occupied, TILE - 1, 0)[0:8] < 0.5 * EMPTY
    back = jnp.where(occupied, back, 0)
    root = pltpu.roll(OWN[4], TILE - 1, 0)[0:8]
    values = [RES[i] * FORCE for i in range(3)] + [RES[3] * (0.5 * PHI) - 1.0 - root]
    for i, value in enumerate(values):
        value = jnp.where(occupied, across(value, back), 0.0)
        for half, part in enumerate((value, pltpu.roll(value, SLOTS, 1))):
            if i < 3:
                force[i, half] = part[:, :SLOTS]
            else:
                energy[half] = part[:, :SLOTS]


def local_step(at_z, recv, interpret=False):
    consts = [jnp.asarray(c) for c in constants()]
    vmem = pl.BlockSpec(memory_space=pltpu.VMEM)
    return pl.pallas_call(
        kernel,
        out_shape=(
            jax.ShapeDtypeStruct((3, 2, 8, SLOTS), f32),
            jax.ShapeDtypeStruct((2, 8, SLOTS), f32),
        ),
        in_specs=[pl.BlockSpec(memory_space=pltpu.SMEM)] + [vmem] * 7,
        out_specs=(vmem, vmem),
        scratch_shapes=[
            pltpu.VMEM((8, 256), jnp.int32),
            pltpu.VMEM((256, 256), bf16),
            pltpu.VMEM((256, 256), f32),
            pltpu.SMEM((8, 256), jnp.int32),
            pltpu.SMEM((LAYERS + 1, TILE), jnp.int32),
            pltpu.VMEM((LAYERS, 3, TILE, 256), f32),
            pltpu.VMEM((LAYERS * 256, DEPTH), bf16),
            pltpu.VMEM((NY + 2, CAPACITY, TERMS), bf16),
            pltpu.VMEM((MIDDLE, NY, 2, TERMS, 128), bf16),
            pltpu.VMEM((MIDDLE, 3, 2, TILE, 128), f32),
            pltpu.VMEM((MIDDLE, 2, TILE, 128), f32),
            pltpu.VMEM((MIDDLE, 2, TILE, 128), f32),
            pltpu.VMEM((5, TILE, 128), f32),
            pltpu.VMEM((4, TILE, 128), f32),
            pltpu.VMEM((8, 128, 128), f32),
            pltpu.VMEM((8, 128, 512), f32),
            pltpu.VMEM((4, 8, 128), f32),
            pltpu.SemaphoreType.DMA,
        ],
        compiler_params=pltpu.CompilerParams(vmem_limit_bytes=48 * 2**20),
        interpret=interpret,
    )(at_z, recv, *consts)


def along(axis, distance):
    n = lax.axis_size(axis)
    return [(i, (i + distance) % n) for i in range(n)]


def marking_kernel(counts, positions, own, up, down):
    lane = lax.broadcasted_iota(jnp.int32, (1, SLOTS), 1)
    for i in range(2):
        lanes = slice(SLOTS * i, SLOTS * (i + 1))
        for j in range(8):
            row = jnp.where(lane < counts[0, i, j], positions[0, 0, i, j : j + 1, :], FAR)
            own[0, j : j + 1, lanes] = row
        for c in (1, 2):
            own[c, :, lanes] = positions[c, 0, i]
    for c in range(3):
        up[c] = own[c, 7:8]
        down[c] = own[c, 0:1]


def marked(positions, counts):
    vmem = pl.BlockSpec(memory_space=pltpu.VMEM)
    return pl.pallas_call(
        marking_kernel,
        out_shape=tuple(jax.ShapeDtypeStruct((3, n, 128), f32) for n in (8, 1, 1)),
        in_specs=[pl.BlockSpec(memory_space=pltpu.SMEM), vmem],
        out_specs=(vmem,) * 3,
    )(counts, positions)


def spreading_kernel(before, own, after, out):
    rows = [jnp.concatenate([before[c], own[c], after[c]], axis=1) for c in range(3)]
    layer = jnp.concatenate(rows + [jnp.zeros((2, 256), f32)], axis=0)
    for k in range(out.shape[0]):
        out[k] = layer


def spread(before, own, after, copies):
    vmem = pl.BlockSpec(memory_space=pltpu.VMEM)
    return pl.pallas_call(
        spreading_kernel,
        out_shape=jax.ShapeDtypeStruct((copies, 32, 256), f32),
        in_specs=[vmem] * 3,
        out_specs=vmem,
    )(before, own, after)


def gathered(positions, counts):
    nz = lax.axis_size("gz")
    own, up, down = marked(positions, counts)
    before = lax.ppermute(up, "gy", along("gy", 1))
    after = lax.ppermute(down, "gy", along("gy", -1))
    own = jnp.concatenate([before, own, after], axis=1)
    before = lax.ppermute(own[..., 64:], "gx", along("gx", 1))
    after = lax.ppermute(own[..., :64], "gx", along("gx", -1))
    recv = lax.all_to_all(spread(before, own, after, nz), "gz", 0, 0)
    return lax.axis_index("gz").astype(jnp.int32).reshape(1), recv


def body(positions, counts):
    force, energy = local_step(*gathered(positions, counts))
    return force[:, None], energy[None]


def solution(mesh):
    return jax.shard_map(
        body,
        mesh=mesh,
        in_specs=(P(None, "gz", "gx", "gy", None), P("gz", "gx", "gy")),
        out_specs=(P(None, "gz", "gx", "gy", None), P("gz", "gx", "gy", None)),
        check_vma=False,
    )
```

```python
import functools
import math

import jax
import jax.numpy as jnp
import ml_dtypes
import numpy as np
from jax import lax
from jax.experimental import pallas as pl
from jax.experimental.pallas import tpu as pltpu
from jax.sharding import PartitionSpec as P

SLOTS = 64
FAR = 100.0

cutoff_sq = 4.95 * 4.95
side_xy, side_z = 12.0, 2.5
KAPPA = math.log2(math.e) / 8.0
UNIT = math.sqrt(KAPPA)
TOP = KAPPA * cutoff_sq
RATIO = 8.0 / 3.0
DENSITY = 2.0 ** (-TOP) / TOP**2
PAIR = 2.0 ** (-TOP * RATIO)
G, H = 8.0 * 2.0 * TOP / cutoff_sq, 3.0 * 2.0 * TOP / cutoff_sq
FORCE = 4.0 * PAIR / (3.0 * TOP * TOP) / UNIT
SLOPE = 2.0 * 2.0 ** (-TOP) / (8.0 * TOP * TOP) / (FORCE * UNIT)
PHI = 2.0 * PAIR / TOP**2

NY = 10
TILE = 16
LAYERS, MIDDLE = 9, 5
TERMS = 32
DEPTH = 13 * TILE
WINDOW, EDGE, EXTRA = 768, 576, 128
STEP = 32
CAPACITY = LAYERS * 256 + WINDOW + EXTRA
EMPTY = FAR * side_xy * UNIT
BOX = (side_xy * UNIT, 4 * side_xy * UNIT, 0.5 * side_z * UNIT)
NEAR = TOP * 1.001
f32, bf16 = jnp.float32, jnp.bfloat16


def constants():
    sel_b = np.zeros((NY, TERMS, DEPTH), np.float32)
    sel_a = np.zeros((NY, TERMS, DEPTH), np.float32)
    tops = []
    rest = np.float32(TOP)
    for _ in range(3):
        piece = rest.astype(ml_dtypes.bfloat16).astype(np.float32)
        tops.append(piece)
        rest = np.float32(rest - piece)
    one = 12 * TILE
    for j in range(NY):
        row = 0
        for c in range(3):
            for pa, pb in ((0, 0), (0, 1), (0, 2), (1, 0), (1, 1), (2, 0)):
                sel_a[j, row, TILE * (3 * c + pa) + j] = 2.0
                sel_b[j, row, TILE * (3 * c + pb) + j] = 1.0
                row += 1
        for p in range(3):
            sel_a[j, row, one] = -1.0
            sel_b[j, row, TILE * (9 + p) + j] = 1.0
            row += 1
            sel_a[j, row, TILE * (9 + p) + j] = -1.0
            sel_b[j, row, one] = 1.0
            row += 1
            sel_a[j, row, one] = tops[p]
            sel_b[j, row, one] = 1.0
            row += 1
    across = np.zeros((DEPTH, NY, 128), np.float32)
    across[:, :, :TERMS] = sel_b.transpose(2, 0, 1)
    outside = np.zeros((WINDOW + EXTRA, TERMS), np.float32)
    outside[:, 18] = 2.0**14
    lane = np.arange(256)
    cast = lambda x: x.astype(ml_dtypes.bfloat16)
    return (
        cast(across.reshape(DEPTH, NY * 128)),
        cast(sel_a.reshape(NY * TERMS, DEPTH)),
        cast(np.eye(256, dtype=np.float32)),
        cast((lane[:, None] <= lane[None, :]).astype(np.float32)),
        cast(outside),
        cast((np.arange(512)[:, None] // 128 == lane[None, :128]).astype(np.float32)),
    )


def split3(x):
    a = x.astype(bf16)
    r = x - a.astype(f32)
    b = r.astype(bf16)
    c = (r - b.astype(f32)).astype(bf16)
    return (a, b, c)


def pieces(x, y, z):
    parts = split3(x) + split3(y) + split3(z) + split3(x * x + y * y + z * z)
    return jnp.concatenate(parts + (jnp.ones((TILE, x.shape[1]), bf16),), axis=0)


def across(x, index):
    return jnp.take_along_axis(x, index, axis=1)


def taken(x, index):
    low = across(x[:, :128], index & 127)
    high = across(x[:, 128:], index & 127)
    return jnp.where(index >= 128, high, low)


def packed(count, fields, group):
    place = lax.broadcasted_iota(jnp.int32, (TILE, 128), 1) + 128 * group
    want = place.astype(f32)
    low, high = count[:, :128], count[:, 128:]
    beyond = want >= low[:, 127:128]
    at = jnp.zeros((TILE, 128), jnp.int32)
    for step in (64, 32, 16, 8, 4, 2, 1):
        probe = at + (step - 1)
        seen = across(high, probe)
        if group == 0:
            seen = jnp.where(beyond, seen, across(low, probe))
        at = jnp.where(seen <= want, at + step, at)
    there = want < high[:, 127:128]
    found = []
    for field, blank in zip(fields, (EMPTY, 0.0, 0.0)):
        value = across(field[:, 128:], at)
        if group == 0:
            value = jnp.where(beyond, value, across(field[:, :128], at))
        found.append(jnp.where(there, value, blank))
    return found


def push_parts(centre, partner, sums):
    (xp, yp, zp, sp), (xq, yq, zq, sq), (fx, fy, fz, ph) = centre, partner, sums
    dx, dy, dz = xp - xq, yp - yq, zp - zq
    tau = jnp.maximum(TOP - (dx * dx + dy * dy + dz * dz), 0.0)
    w = jnp.exp2(tau * RATIO) * tau
    push = (sp + sq) * (jnp.exp2(tau) * tau * (tau + G)) + w * (tau + H)
    return fx + push * dx, fy + push * dy, fz + push * dz, ph + w * tau


def kernel(
    at_z, recv, place_b, sel_a, eye, upto, outside, add_up, force, energy,
    COUNT, MASK, CUM, NUMS, OFF, XYZ, TURNED, P, C, D, SLOPE_D, ROOT_D, OWN, LATE, COL, SUM, RES, sem,
):
    SLOPE_D[...] = jnp.ones(SLOPE_D.shape, f32)
    row = lax.broadcasted_iota(jnp.int32, (TILE, 256), 0)
    cell = lax.broadcasted_iota(jnp.int32, (TILE, 256), 1) // SLOTS
    real = row < NY
    ring = recv.shape[0]

    for l in range(LAYERS):
        raw = recv[lax.rem(at_z[0] + (l + ring - 4), ring)]
        x = (raw[0:TILE] + (cell - 2).astype(f32)) * (side_xy * UNIT)
        y = (pltpu.roll(raw, 32 - NY, 0)[0:TILE] + (row - 5).astype(f32)) * (side_xy * UNIT)
        z = (pltpu.roll(raw, 32 - 2 * NY, 0)[0:TILE] + (l - 4.5)) * (side_z * UNIT)
        for c, value in enumerate((x, y, z)):
            XYZ[l, c] = value
        apart = [jnp.maximum(jnp.abs(v) - side, 0.0) for v, side in zip((x, y, z), BOX)]
        far = apart[0] * apart[0] + apart[1] * apart[1] + apart[2] * apart[2]
        mark = lambda test: jnp.where(real & test, 1.0, 0.0).astype(bf16)
        MASK[TILE * l : TILE * (l + 1)] = mark(far < 4.0 * NEAR)
        if 2 <= l <= 6:
            MASK[TILE * (l + 7) : TILE * (l + 8)] = mark(far < NEAR)
        if l == 4:
            inside = (cell >= 1) & (cell <= 2) & (row >= 1) & (row <= 8) & (x < 0.5 * EMPTY)
            MASK[TILE * 14 : TILE * 15] = mark(inside)
            MASK[TILE * 15 : TILE * 16] = jnp.zeros((TILE, 256), bf16)
    CUM[...] = jnp.dot(MASK[...], upto[...], preferred_element_type=f32)
    COUNT[...] = lax.dot_general(
        jnp.ones((8, 256), bf16), MASK[...], (((1,), (1,)), ((), ())), preferred_element_type=f32
    ).astype(jnp.int32)
    copy = pltpu.make_async_copy(COUNT, NUMS, sem)
    copy.start()

    for l in range(MIDDLE):
        count = CUM[TILE * (l + 9) : TILE * (l + 10)]
        fields = [XYZ[l + 2, c] for c in range(3)]
        lists = [packed(count, fields, w) for w in range(2)]
        for w in range(2):
            for c in range(3):
                D[l, c, w] = lists[w][c]
        both = jnp.concatenate([pieces(*lists[w]) for w in range(2)], axis=1)
        terms = jnp.dot(sel_a[...], both, preferred_element_type=f32).astype(bf16)
        for j in range(NY):
            for w in range(2):
                C[l, j, w] = terms[TERMS * j : TERMS * (j + 1), 128 * w : 128 * (w + 1)]
    copy.wait()

    for j in range(NY + 2):
        start = jnp.int32(0)
        for l in range(LAYERS):
            OFF[l, j] = start
            if 1 <= j <= NY:
                start = start + ((NUMS[0, TILE * l + j - 1] + 15) >> 4 << 4)
        OFF[LAYERS, j] = start
    for l in range(LAYERS):
        count = CUM[TILE * l : TILE * (l + 1)]
        fields = [XYZ[l, c] for c in range(3)]
        both = [pieces(*packed(count, fields, w)) for w in range(2)]
        TURNED[256 * l : 256 * (l + 1)] = lax.dot_general(
            eye[...],
            jnp.concatenate(both, axis=1),
            (((1,), (1,)), ((), ())),
            preferred_element_type=f32,
        ).astype(bf16)
    for j in range(NY):
        place = place_b[:, 128 * j : 128 * (j + 1)]
        rows = jnp.dot(TURNED[...], place, preferred_element_type=f32)[:, :TERMS].astype(bf16)
        for l in range(LAYERS):
            start = pl.multiple_of(OFF[l, j + 1], 16)
            P[j + 1, pl.ds(start, 256), :] = rows[256 * l : 256 * (l + 1)]
    for j in range(NY + 2):
        P[j, pl.ds(pl.multiple_of(OFF[LAYERS, j], 16), WINDOW + EXTRA), :] = outside[...]

    def density(rows, lanes):
        tau = jnp.maximum(jnp.dot(rows, lanes, preferred_element_type=f32), 0.0)
        value = tau * tau * jnp.exp2(tau)
        return jnp.sum(value.reshape(-1, 8, 128), axis=0)

    def summed(l, j, w):
        total = jnp.zeros((8, 128), f32)
        for k in range(max(j - 1, 0), min(j + 2, NY)):
            window = EDGE if k in (0, NY - 1) else WINDOW
            start = pl.multiple_of(OFF[l, k + 1], 16)
            total = total + density(P[k + 1, pl.ds(start, window), :], C[l, j, w])
        SLOPE_D[l, w, j : j + 1, :] = jnp.sum(total, axis=0, keepdims=True)

    def rest(l, j, w):
        total = jnp.zeros((8, 128), f32)
        for k in range(max(j - 1, 0), min(j + 2, NY)):
            start = OFF[l, k + 1] + (EDGE if k in (0, NY - 1) else WINDOW)
            more = jnp.maximum(OFF[l + MIDDLE, k + 1] - start + EXTRA - 1, 0) // EXTRA

            def further(i, total):
                at = pl.multiple_of(start + i * EXTRA, 16)
                return total + density(P[k + 1, pl.ds(at, EXTRA), :], C[l, j, w])

            total = lax.fori_loop(0, more, further, total)
        SLOPE_D[l, w, j : j + 1, :] += jnp.sum(total, axis=0, keepdims=True)

    @pl.loop(0, MIDDLE)
    def _(l):
        for j in range(NY):
            summed(l, j, 0)
        excess = []
        for k in range(NY):
            length = OFF[l + MIDDLE, k + 1] - OFF[l, k + 1]
            excess.append(length - (EDGE if k in (0, NY - 1) else WINDOW))
        for j in range(NY):
            many = NUMS[0, TILE * (l + 9) + j] > 128

            @pl.when(many)
            def _():
                summed(l, j, 1)

            most = functools.reduce(jnp.maximum, excess[max(j - 1, 0) : min(j + 2, NY)])

            @pl.when(most > 0)
            def _():
                @pl.loop(0, jnp.where(many, 2, 1))
                def _(w):
                    rest(l, j, w)

    root = jnp.sqrt(jnp.maximum(SLOPE_D[...] * DENSITY, 0.5))
    ROOT_D[...] = root
    SLOPE_D[...] = (-0.5 * SLOPE) / root

    count = CUM[TILE * 11 : TILE * 12]
    before = count[:, SLOTS - 1 : SLOTS].astype(jnp.int32)
    index = lax.broadcasted_iota(jnp.int32, (TILE, 128), 1) + before
    for c, pair in enumerate(
        [[D[2, c, w] for w in range(2)] for c in range(3)]
        + [[A[2, w] for w in range(2)] for A in (SLOPE_D, ROOT_D)]
    ):
        OWN[c] = taken(jnp.concatenate(pair, axis=1), index)

    start = jnp.zeros((TILE, 1), f32)
    place = lax.broadcasted_iota(jnp.int32, (TILE, 128), 1)
    for c in range(4):
        LATE[c] = jnp.full((TILE, 128), EMPTY if c == 0 else 0.0, f32)
    for l in range(MIDDLE):
        held = jnp.maximum(CUM[TILE * (l + 9) : TILE * (l + 10), 255:256] - 128.0, 0.0)
        held = jnp.broadcast_to(held, (TILE, 128))
        for side in range(3):
            n = pltpu.roll(held, (TILE + 1 - side) % TILE, 0)
            first = jnp.broadcast_to(start, (TILE, 128))
            ours = (place.astype(f32) >= first) & (place.astype(f32) < first + n)
            index = (place - first.astype(jnp.int32)) & 127
            for c, field in enumerate([D[l, c, 1] for c in range(3)] + [SLOPE_D[l, 1]]):
                field = pltpu.roll(field, (TILE + 1 - side) % TILE, 0)
                LATE[c] = jnp.where(ours, across(field, index), LATE[c])
            start = start + n[:, 0:1]
    inner = lax.broadcasted_iota(jnp.int32, (TILE, 1), 0)
    inner = (inner >= 1) & (inner <= 8)
    crowded = jnp.max(jnp.where(inner, start, 0.0)) > 128.0

    @pl.when(crowded)
    def _():
        LATE[0] = jnp.full((TILE, 128), EMPTY, f32)

    def partner(l, j, w):
        one = pl.ds(j, 1)
        return (D[l, 0, w, one, :], D[l, 1, w, one, :], D[l, 2, w, one, :], SLOPE_D[l, w, one, :])

    def centre(j, rows):
        cols = COL[j, rows, :]
        return tuple(jnp.broadcast_to(cols[:, i : i + 1], (STEP, 128)) for i in range(4))

    def steps(j):
        return (NUMS[0, TILE * 14 + j + 1] + STEP - 1) // STEP

    @pl.loop(0, 8)
    def _(j):
        stack = jnp.concatenate([OWN[c, pl.ds(j + 1, 1), :] for c in range(4)] * 2, axis=0)
        COL[j, :, 0:8] = stack.T

        @pl.loop(0, steps(j))
        def _(g):
            rows = pl.ds(pl.multiple_of(g * STEP, STEP), STEP)
            mine = centre(j, rows)
            sums = (jnp.zeros((STEP, 128), f32),) * 4
            for l in range(MIDDLE):
                for side in range(3):
                    sums = push_parts(mine, partner(l, j + side, 0), sums)
            late = tuple(LATE[c, pl.ds(j + 1, 1), :] for c in range(4))
            sums = push_parts(mine, late, sums)
            for i in range(4):
                SUM[j, rows, 128 * i : 128 * (i + 1)] = sums[i]

    @pl.when(crowded)
    def _():
        @pl.loop(0, MIDDLE)
        def _(l):
            @pl.loop(0, NY)
            def _(k):
                some = jnp.where(NUMS[0, TILE * (l + 9) + k] > 128, 1, 0)

                @pl.loop(jnp.maximum(k - 2, 0), jnp.minimum(k + 1, 8))
                def _(j):
                    @pl.loop(0, steps(j) * some)
                    def _(g):
                        rows = pl.ds(pl.multiple_of(g * STEP, STEP), STEP)
                        sums = tuple(SUM[j, rows, 128 * i : 128 * (i + 1)] for i in range(4))
                        sums = push_parts(centre(j, rows), partner(l, k, 1), sums)
                        for i in range(4):
                            SUM[j, rows, 128 * i : 128 * (i + 1)] = sums[i]

    total = jnp.zeros((8 * 128, 128), f32)
    for part in split3(SUM[...].reshape(8 * 128, 4 * 128))[:2]:
        total = total + jnp.dot(part, add_up[...], preferred_element_type=f32)
    for j in range(8):
        across_lanes = total[128 * j : 128 * (j + 1), 0:8].T
        for i in range(4):
            RES[i, j : j + 1, :] = across_lanes[i : i + 1]

    back = pltpu.roll(count, 256 - SLOTS, 1)[:, :128].astype(jnp.int32) - 1 - before
    back = jnp.concatenate([pltpu.roll(back, TILE - 1, 0)[0:8]], axis=0)
    occupied = pltpu.roll(XYZ[4, 0], 256 - SLOTS, 1)[:, :128]
    occupied = pltpu.roll(occupied, TILE - 1, 0)[0:8] < 0.5 * EMPTY
    back = jnp.where(occupied, back, 0)
    root = pltpu.roll(OWN[4], TILE - 1, 0)[0:8]
    values = [RES[i] * FORCE for i in range(3)] + [RES[3] * (0.5 * PHI) - 1.0 - root]
    for i, value in enumerate(values):
        value = jnp.where(occupied, across(value, back), 0.0)
        for half, part in enumerate((value, pltpu.roll(value, SLOTS, 1))):
            if i < 3:
                force[i, half] = part[:, :SLOTS]
            else:
                energy[half] = part[:, :SLOTS]


def local_step(at_z, recv, interpret=False):
    consts = [jnp.asarray(c) for c in constants()]
    vmem = pl.BlockSpec(memory_space=pltpu.VMEM)
    return pl.pallas_call(
        kernel,
        out_shape=(
            jax.ShapeDtypeStruct((3, 2, 8, SLOTS), f32),
            jax.ShapeDtypeStruct((2, 8, SLOTS), f32),
        ),
        in_specs=[pl.BlockSpec(memory_space=pltpu.SMEM)] + [vmem] * 7,
        out_specs=(vmem, vmem),
        scratch_shapes=[
            pltpu.VMEM((8, 256), jnp.int32),
            pltpu.VMEM((256, 256), bf16),
            pltpu.VMEM((256, 256), f32),
            pltpu.SMEM((8, 256), jnp.int32),
            pltpu.SMEM((LAYERS + 1, TILE), jnp.int32),
            pltpu.VMEM((LAYERS, 3, TILE, 256), f32),
            pltpu.VMEM((LAYERS * 256, DEPTH), bf16),
            pltpu.VMEM((NY + 2, CAPACITY, TERMS), bf16),
            pltpu.VMEM((MIDDLE, NY, 2, TERMS, 128), bf16),
            pltpu.VMEM((MIDDLE, 3, 2, TILE, 128), f32),
            pltpu.VMEM((MIDDLE, 2, TILE, 128), f32),
            pltpu.VMEM((MIDDLE, 2, TILE, 128), f32),
            pltpu.VMEM((5, TILE, 128), f32),
            pltpu.VMEM((4, TILE, 128), f32),
            pltpu.VMEM((8, 128, 128), f32),
            pltpu.VMEM((8, 128, 512), f32),
            pltpu.VMEM((4, 8, 128), f32),
            pltpu.SemaphoreType.DMA,
        ],
        compiler_params=pltpu.CompilerParams(vmem_limit_bytes=48 * 2**20),
        interpret=interpret,
    )(at_z, recv, *consts)


def along(axis, distance):
    n = lax.axis_size(axis)
    return [(i, (i + distance) % n) for i in range(n)]


def marking_kernel(counts, positions, own, up, down):
    lane = lax.broadcasted_iota(jnp.int32, (1, SLOTS), 1)
    for i in range(2):
        lanes = slice(SLOTS * i, SLOTS * (i + 1))
        for j in range(8):
            row = jnp.where(lane < counts[0, i, j], positions[0, 0, i, j : j + 1, :], FAR)
            own[0, j : j + 1, lanes] = row
        for c in (1, 2):
            own[c, :, lanes] = positions[c, 0, i]
    for c in range(3):
        up[c] = own[c, 7:8]
        down[c] = own[c, 0:1]


def marked(positions, counts):
    vmem = pl.BlockSpec(memory_space=pltpu.VMEM)
    return pl.pallas_call(
        marking_kernel,
        out_shape=tuple(jax.ShapeDtypeStruct((3, n, 128), f32) for n in (8, 1, 1)),
        in_specs=[pl.BlockSpec(memory_space=pltpu.SMEM), vmem],
        out_specs=(vmem,) * 3,
    )(counts, positions)


def gathered(positions, counts):
    nz = lax.axis_size("gz")
    own, up, down = marked(positions, counts)
    before = lax.ppermute(up, "gy", along("gy", 1))
    after = lax.ppermute(down, "gy", along("gy", -1))
    own = jnp.concatenate([before, own, after], axis=1)
    before = lax.ppermute(own[..., 64:], "gx", along("gx", 1))
    after = lax.ppermute(own[..., :64], "gx", along("gx", -1))
    own = jnp.concatenate([before, own, after], axis=2).reshape(30, 256)
    own = jnp.pad(own, ((0, 2), (0, 0)))
    recv = lax.all_to_all(jnp.broadcast_to(own, (nz, 32, 256)), "gz", 0, 0)
    return lax.axis_index("gz").astype(jnp.int32).reshape(1), recv


def body(positions, counts):
    force, energy = local_step(*gathered(positions, counts))
    return force[:, None], energy[None]


def solution(mesh):
    return jax.shard_map(
        body,
        mesh=mesh,
        in_specs=(P(None, "gz", "gx", "gy", None), P("gz", "gx", "gy")),
        out_specs=(P(None, "gz", "gx", "gy", None), P("gz", "gx", "gy", None)),
        check_vma=False,
    )
```
